256 devices in a mesh: sub: 64 (over y, z, core), inner: 4 (over x).
Axes of the slice: x: 4, y: 4, z: 8, core: 2. Of those that a mesh axis runs over, the one named last changes fastest.
Arguments:
- blocks: bfloat16 [16384, 2, 128, 128], P(('sub', 'inner')), may hold values from -6 to 6
- routes: int32 [16384, 1], P(('sub', 'inner')), may hold values from 0 to 63; in each aligned block of 64 rows (0 to 63, 64 to 127, ...) at most 2 rows name the same one
- offsets: int32 [16384, 2], P(('sub', 'inner')), may hold values from 0 to 203
- live: int32 [16384], P(('sub', 'inner')), may hold values from 32 to 128
- start_modes: bfloat16 [64, 204, 64, 128], P('sub', None, 'inner'), may hold values from -6 to 6
Outputs:
- modes: bfloat16 [64, 204, 64, 128], P('sub', None, 'inner')
- ritz: float32 [64, 64, 64], P('sub')
The draws below stay inside these ranges and needn't reach their ends.
Inputs may be any that keep to these rules, and one draw needn't show every extreme that they name: `routes`: among the 64 row blocks of one device at most 2 name the same subdomain.
All inputs are finite; a program needn't handle non-finite values.
Results may differ from the reference program's by a relative error of at most 0.025.
Values may be sent and summed in bfloat16 or wider, within the bound.
No kernel may reach another device: no remote copies, remote signals or barrier semaphores. Data moves between devices by JAX's collectives and lax.ppermute only.
A program may use at most 128 MiB of HBM per device.

```python
import math
import jax
import jax.numpy as jnp
import numpy as np
from jax import lax

BLK = 128
CB = 196
DB = 204
K = 2
M = 64
RB = 64
ITERS = 3
CAP = 2
RBALL = 16384
N_SUB = 64
N_INNER = 4


def plant(drawn, own_key, least, top_value):
    dims = drawn.shape
    place = [jax.random.randint(jax.random.fold_in(own_key, axis), (), 0, dims[axis]) for axis in range(len(dims))]
    drawn = drawn.at[tuple(place)].set(least)
    longest = dims.index(max(dims))
    place[longest] = (place[longest] + 1) % dims[longest]
    return drawn.at[tuple(place)].set(top_value)


def shard_levels(key, extent, pieces, least, largest):
    loudness, own = 1.0, jax.random.fold_in(key, 6)
    for position, parts in pieces:
        heights = jnp.exp(jax.random.uniform(jax.random.fold_in(own, position), (parts,), jnp.float32, least / len(pieces), largest / len(pieces)))
        loudness = loudness * jnp.repeat(heights, extent[position] // parts).reshape([-1 if axis == position else 1 for axis in range(len(extent))])
    return loudness


def deal_out(key, own, number, rows, number_of, top, most, lean):
    sequence = jax.random.permutation(key, number_of)
    heavy_load, common = load_shares(number_of, rows * top, most, lean, True), load_shares(number_of, rows * top, most, lean, False)
    places = jnp.arange(number_of)

    def named(lengths, offset_by):
        used = int((lengths > 0).sum())
        fixed = max(1, used // 4)
        shifted = fixed + (places - fixed + offset_by * (used - fixed)) % max(1, number_of - fixed)
        return jnp.zeros((number_of,), jnp.int32).at[sequence[jnp.where(places < fixed, places, shifted)]].set(jnp.asarray(lengths, jnp.int32))

    lengths = jnp.where(number % 4 == 0, named(heavy_load, number // 4), named(common, number - number // 4 - 1))
    mixed = jax.random.permutation(jax.random.fold_in(own, 3), number_of)
    source_of, receiver = mixed[0:number_of // 2 * 2:2], mixed[1:number_of // 2 * 2:2]
    room = jnp.minimum(lengths[source_of] - 1, most - lengths[receiver]) // 2
    room = jnp.where((source_of == sequence[0]) | (receiver == sequence[0]) | (lengths[receiver] == 0), 0, jnp.maximum(room, 0))
    shifted = jax.random.randint(jax.random.fold_in(own, 4), (number_of // 2,), 0, 1 << 20) % (room + 1)
    lengths = lengths.at[source_of].add(-shifted).at[receiver].add(shifted)
    labels = jnp.searchsorted(jnp.cumsum(lengths), jnp.arange(rows * top), side="right").astype(jnp.int32)
    table = labels.reshape(top, rows).T
    table = table[jax.random.permutation(jax.random.fold_in(own, 1), rows)]
    offset_by = jax.random.randint(jax.random.fold_in(own, 2), (rows, 1), 0, top)
    return jnp.take_along_axis(table, (jnp.arange(top)[None, :] + offset_by) % top, axis=1)


def load_shares(number_of, total, reach, slope, full):
    weights = [(1 << 20) // math.isqrt(grade ** slope) + 1 for grade in range(1, number_of + 1)]
    largest = reach if full else min(reach, max(-(-total // number_of), total * weights[0] // sum(weights)))
    least = 1 if total - largest >= number_of - 1 else 0
    given, rest = [largest] + [least] * (number_of - 1), total - largest - least * (number_of - 1)
    while rest > 0:
        free = [i for i in range(1, number_of) if given[i] < largest] or [i for i in range(1, number_of) if given[i] < reach]
        mass, left = sum([weights[i] for i in free]), rest
        for i in free:
            more = min(reach - given[i], max(1, left * weights[i] // mass), rest)
            given[i] = given[i] + more
            rest = rest - more
    return np.array(given)


def bell_draw(own_key, dims, width, bound, split=(), kind=jnp.bfloat16):
    drawn = jax.random.normal(own_key, dims, jnp.float32) * width
    if len(split) > 0:
        drawn = shard_levels(own_key, dims, split, -0.22, 0.18) * drawn
    return jnp.clip(drawn, min=-bound, max=bound).astype(kind)


def setup_inputs(seed: int = 0) -> dict:
    arg_keys = jax.random.split(jax.random.key(seed), 6)
    blocks = bell_draw(arg_keys[0], (RBALL, K, BLK, BLK), 1.0, 6.0, ((0, 256),))
    routes_keys = jax.random.split(jax.random.fold_in(arg_keys[1], 1), RBALL // RB)
    routes_turns = jax.random.permutation(jax.random.fold_in(arg_keys[1], 3), RBALL // RB)
    routes = jax.vmap(lambda own, number: deal_out(jax.random.fold_in(arg_keys[1], 2), own, number, RB, N_SUB, 1, CAP, 2))(routes_keys, routes_turns).reshape((RBALL, 1))
    offsets = plant(jax.random.randint(arg_keys[2], (RBALL, K), 0, DB), jax.random.fold_in(arg_keys[2], 1), 0, DB - 1).astype(jnp.int32)
    live = plant(jax.random.randint(arg_keys[3], (RBALL,), BLK // 4, BLK + 1), jax.random.fold_in(arg_keys[3], 1), BLK // 4, BLK).astype(jnp.int32)
    start_modes = bell_draw(arg_keys[4], (N_SUB, DB, M, BLK), 1.0, 6.0, ((0, 64), (2, 4)))
    return dict(blocks=blocks, routes=routes, offsets=offsets, live=live, start_modes=start_modes)


DAMPING = 32.0

def orthonormal(applied):
    wide = applied.astype(jnp.float32)
    gram = jnp.einsum('dmc,dnc->mn', wide, wide)
    lower = jnp.linalg.cholesky(gram)
    inverse = lax.linalg.triangular_solve(lower, jnp.eye(M, dtype=jnp.float32), left_side=True, lower=True)
    rounded = inverse.astype(jnp.bfloat16).astype(jnp.float32)
    return jnp.einsum('dnc,mn->dmc', wide, rounded, precision=lax.Precision.HIGHEST).astype(jnp.bfloat16)

def reference(blocks, routes, offsets, live, start_modes):
    subs = N_SUB
    inners = N_INNER
    total_cols = CB * subs
    devices_all = subs * inners
    targets = routes[:, 0].astype(jnp.int32)
    column_ids = ((targets[:, None] * CB + offsets) % total_cols).astype(jnp.int32)
    live_rows = (jnp.arange(BLK, dtype=jnp.int32)[None, :] < live[:, None]).astype(jnp.float32)

    def square_sums(pair):
        part_blocks, part_live = pair
        as_float = part_blocks.astype(jnp.float32)
        return jnp.einsum('skrc,sr->skc', as_float * as_float, part_live)
    column_part = lax.map(square_sums, (blocks.reshape(devices_all, RB, K, BLK, BLK), live_rows.reshape(devices_all, RB, BLK)))
    column_part = column_part.reshape(RB * devices_all, K, BLK)
    column_sq = jnp.zeros((total_cols, BLK), jnp.float32).at[column_ids].add(column_part)
    scale = lax.rsqrt(column_sq + DAMPING)
    domain_ids = ((jnp.arange(subs, dtype=jnp.int32)[:, None] * CB + jnp.arange(DB, dtype=jnp.int32)[None, :]) % total_cols).astype(jnp.int32)
    damped = DAMPING * scale[domain_ids] * scale[domain_ids]
    block_scale = scale[column_ids].reshape(subs, inners, RB, K, BLK)
    device_blocks = blocks.reshape(subs, inners, RB, K, BLK, BLK)
    device_live = live_rows.reshape(subs, inners, RB, BLK)
    device_targets = targets.reshape(subs, inners, RB)
    device_offsets = offsets.reshape(subs, inners, RB, K)

    def apply_rows(current):
        total = jnp.zeros((subs, DB, M, BLK), jnp.float32)
        for inner_j in range(inners):

            def add_device(carry, items):
                part_blocks, part_live, part_scale, part_targets, part_offsets = items
                scaled = (part_blocks.astype(jnp.float32) * part_live[:, None, :, None] * part_scale[:, :, None, :]).astype(jnp.bfloat16)
                picked = current[part_targets[:, None], part_offsets]
                projected = jnp.einsum('skrc,skmc->smr', scaled.astype(jnp.float32), picked.astype(jnp.float32)).astype(jnp.bfloat16)
                spread = jnp.einsum('skrc,smr->skmc', scaled.astype(jnp.float32), projected.astype(jnp.float32))
                return (carry.at[part_targets[:, None], part_offsets].add(spread), None)
            partial_value, _ = lax.scan(add_device, jnp.zeros((subs, DB, M, BLK), jnp.float32), (device_blocks[:, inner_j], device_live[:, inner_j], block_scale[:, inner_j], device_targets[:, inner_j], device_offsets[:, inner_j]))
            rounded = lax.optimization_barrier(partial_value.astype(jnp.bfloat16))
            total = total + rounded.astype(jnp.float32)
        return total
    current = start_modes
    ritz = jnp.zeros((subs, M, M), jnp.float32)
    for step in range(ITERS):
        applied = (apply_rows(current) + damped[:, :, None, :] * current.astype(jnp.float32)).astype(jnp.bfloat16)
        if step == ITERS - 1:
            ritz = jnp.einsum('sdmc,sdnc->smn', current.astype(jnp.float32), applied.astype(jnp.float32))
        current = lax.map(orthonormal, applied)
    return (current, ritz)
```

```python
import functools

import jax
import jax.numpy as jnp
from jax import lax
from jax.experimental import pallas as pl
from jax.experimental.pallas import tpu as pltpu
from jax.sharding import Mesh
from jax.sharding import PartitionSpec as P

OV = 8
ITERS = 3
BLK = 128
DAMPING = 32.0
AXES = ("y", "z", "c", "xh", "xl")
NT = (((1,), (1,)), ((), ()))
VMEM_LIMIT = 50 * 2**20


def nt_dot(left, right):
    return lax.dot_general(left, right, NT, preferred_element_type=jnp.float32)


def pack_kernel(order, blocks, packed, sems):
    slots = packed.shape[0]

    def copy(slot):
        return pltpu.make_async_copy(blocks.at[order[slot]], packed.at[slot], sems.at[slot])

    def start(slot, carry):
        copy(slot).start()
        return carry

    def wait(slot, carry):
        copy(slot).wait()
        return carry

    lax.fori_loop(0, slots, start, 0)
    lax.fori_loop(0, slots, wait, 0)


def pack(blocks, order):
    slots = order.shape[0]
    return pl.pallas_call(
        pack_kernel,
        out_shape=jax.ShapeDtypeStruct((slots,) + blocks.shape[1:], blocks.dtype),
        grid_spec=pltpu.PrefetchScalarGridSpec(
            num_scalar_prefetch=1,
            grid=(1,),
            in_specs=[pl.BlockSpec(memory_space=pl.ANY)],
            out_specs=pl.BlockSpec(memory_space=pl.ANY),
            scratch_shapes=[pltpu.SemaphoreType.DMA((slots,))],
        ),
        compiler_params=pltpu.CompilerParams(vmem_limit_bytes=VMEM_LIMIT),
    )(order, blocks)


def sums_kernel(group, offs, live, blk, sums):
    step = pl.program_id(0)

    @pl.when(step == 0)
    def _():
        sums[...] = jnp.zeros_like(sums)

    rows = lax.broadcasted_iota(jnp.int32, (BLK, BLK), 0)

    def body(s, carry):
        slot = step * group + s
        keep = rows < live[slot]
        for k in range(2):
            wide = blk[s, k].astype(jnp.float32)
            part = jnp.sum(jnp.where(keep, wide * wide, 0.0), axis=0, keepdims=True)
            at = pl.ds(offs[2 * slot + k], 1)
            sums[at, :] = sums[at, :] + part
        return carry

    lax.fori_loop(0, group, body, 0)


def column_sums(blocks, offs, live, domain):
    slots = blocks.shape[0]
    group = min(16, slots)
    return pl.pallas_call(
        functools.partial(sums_kernel, group),
        out_shape=jax.ShapeDtypeStruct((domain, BLK), jnp.float32),
        grid_spec=pltpu.PrefetchScalarGridSpec(
            num_scalar_prefetch=2,
            grid=(slots // group,),
            in_specs=[pl.BlockSpec((group, 2, BLK, BLK), lambda i, *_: (i, 0, 0, 0))],
            out_specs=pl.BlockSpec((domain, BLK), lambda i, *_: (0, 0)),
        ),
        compiler_params=pltpu.CompilerParams(vmem_limit_bytes=VMEM_LIMIT),
    )(offs, live, blocks)


def apply_kernel(first, group, unroll, offs, live, core, blk, scale, own, peer, *rest):
    if first:
        keep, send, scaled, modes, total, sems = rest
    else:
        keep, send, modes, total, sems = rest
    step = pl.program_id(0)
    half = keep.shape[0]
    mine = core[0] * half
    other = (1 - core[0]) * half

    @pl.when(step == 0)
    def _():
        one = pltpu.make_async_copy(own, modes.at[pl.ds(mine, half)], sems.at[0])
        two = pltpu.make_async_copy(peer, modes.at[pl.ds(other, half)], sems.at[1])
        one.start()
        two.start()

        def clear(i, carry):
            total[pl.ds(2 * i, 2)] = jnp.zeros((2,) + total.shape[1:], jnp.float32)
            return carry

        lax.fori_loop(0, half, clear, 0)
        one.wait()
        two.wait()

    rows = lax.broadcasted_iota(jnp.int32, (BLK, BLK), 0)

    def body(g, carry):
        wide, places = [], []
        for u in range(unroll):
            s = g * unroll + u
            slot = step * group + s
            place = [offs[2 * slot], offs[2 * slot + 1]]
            pair = [blk[s, 0], blk[s, 1]]
            if first:
                alive = rows < live[slot]
                for k in range(2):
                    value = pair[k].astype(jnp.float32) * scale[pl.ds(place[k], 1), :]
                    pair[k] = jnp.where(alive, value, 0.0).astype(jnp.bfloat16)
                    scaled[s, k] = pair[k]
            wide.append(jnp.concatenate(pair, axis=1))
            places.append(place)
        picked = [jnp.concatenate([modes[p], modes[q]], axis=1) for p, q in places]
        projected = [nt_dot(v, a).astype(jnp.bfloat16) for v, a in zip(picked, wide)]
        spread = [
            jnp.dot(v, a, preferred_element_type=jnp.float32) for v, a in zip(projected, wide)
        ]
        for (p, q), value in zip(places, spread):
            total[p] += value[:, :BLK]
            total[q] += value[:, BLK:]
        return carry

    lax.fori_loop(0, group // unroll, body, 0)

    @pl.when(step == pl.num_programs(0) - 1)
    def _():
        def write(i, carry):
            keep[pl.ds(2 * i, 2)] = total[pl.ds(mine + 2 * i, 2)].astype(jnp.bfloat16)
            send[pl.ds(2 * i, 2)] = total[pl.ds(other + 2 * i, 2)].astype(jnp.bfloat16)
            return carry

        lax.fori_loop(0, half // 2, write, 0)


def apply_rows(first, blocks, offs, live, core, scale, own, peer):
    slots = blocks.shape[0]
    half, modes, _ = own.shape
    group = min(16, slots)
    unroll = min(8, group)
    block_spec = pl.BlockSpec((group, 2, BLK, BLK), lambda i, *_: (i, 0, 0, 0))
    half_spec = pl.BlockSpec((half, modes, BLK), lambda i, *_: (0, 0, 0))
    half_shape = jax.ShapeDtypeStruct(own.shape, jnp.bfloat16)
    out_shape, out_specs = [half_shape, half_shape], [half_spec, half_spec]
    if first:
        out_shape.append(jax.ShapeDtypeStruct(blocks.shape, jnp.bfloat16))
        out_specs.append(block_spec)
    return pl.pallas_call(
        functools.partial(apply_kernel, first, group, unroll),
        out_shape=out_shape,
        grid_spec=pltpu.PrefetchScalarGridSpec(
            num_scalar_prefetch=3,
            grid=(slots // group,),
            in_specs=[
                block_spec,
                pl.BlockSpec(scale.shape, lambda i, *_: (0, 0)),
                pl.BlockSpec(memory_space=pl.ANY),
                pl.BlockSpec(memory_space=pl.ANY),
            ],
            out_specs=out_specs,
            scratch_shapes=[
                pltpu.VMEM((2 * half, modes, BLK), jnp.bfloat16),
                pltpu.VMEM((2 * half, modes, BLK), jnp.float32),
                pltpu.SemaphoreType.DMA((2,)),
            ],
        ),
        compiler_params=pltpu.CompilerParams(vmem_limit_bytes=VMEM_LIMIT),
    )(offs, live, core, blocks, scale, own, peer)


def image_kernel(with_ritz, one, two, own, damped, applied, gram, *rest):
    step = pl.program_id(0)
    ritz = rest[0] if with_ritz else None

    @pl.when(step == 0)
    def _():
        gram[...] = jnp.zeros_like(gram)
        if with_ritz:
            ritz[...] = jnp.zeros_like(ritz)

    gram_part = jnp.zeros(gram.shape, jnp.float32)
    ritz_part = jnp.zeros(gram.shape, jnp.float32)
    for i in range(0, one.shape[0], 2):
        values, olds = [], []
        for l in (i, i + 1):
            old = own[l]
            total = one[l].astype(jnp.float32) + two[l].astype(jnp.float32)
            value = (total + damped[l] * old.astype(jnp.float32)).astype(jnp.bfloat16)
            applied[l] = value
            values.append(value)
            olds.append(old)
        value = jnp.concatenate(values, axis=1)
        gram_part += nt_dot(value, value)
        if with_ritz:
            ritz_part += nt_dot(jnp.concatenate(olds, axis=1), value)
    gram[...] += gram_part
    if with_ritz:
        ritz[...] += ritz_part


def form_image(with_ritz, one, two, own, damped, steps=3):
    half, modes, _ = own.shape
    part = half // steps
    part_spec = pl.BlockSpec((part, modes, BLK), lambda i: (i, 0, 0))
    square_spec = pl.BlockSpec((modes, modes), lambda i: (0, 0))
    square_shape = jax.ShapeDtypeStruct((modes, modes), jnp.float32)
    squares = 2 if with_ritz else 1
    return pl.pallas_call(
        functools.partial(image_kernel, with_ritz),
        out_shape=[jax.ShapeDtypeStruct(own.shape, jnp.bfloat16)] + [square_shape] * squares,
        grid=(steps,),
        in_specs=[part_spec] * 3 + [pl.BlockSpec((part, 1, BLK), lambda i: (i, 0, 0))],
        out_specs=[part_spec] + [square_spec] * squares,
        compiler_params=pltpu.CompilerParams(vmem_limit_bytes=VMEM_LIMIT),
    )(one, two, own, damped)


def inverse_factor(gram):
    size = gram.shape[0]
    both = (size, 2 * size)
    row_at = lax.broadcasted_iota(jnp.int32, both, 0)
    col_at = lax.broadcasted_iota(jnp.int32, both, 1)
    eye = (col_at == row_at + size).astype(jnp.float32)
    work = jnp.where(col_at < size, jnp.concatenate([gram, gram], axis=1), eye)
    for j in range(size):
        root = lax.rsqrt(work[j : j + 1, j : j + 1])
        row = work[j : j + 1, :] * root
        factor = jnp.where(row_at[:, :1] > j, work[:, j : j + 1] * root, 0.0)
        work = jnp.where(row_at == j, row, work - factor * row)
    return work[:, size:]


def solve_kernel(gram_one, gram_two, applied, new, inverse):
    @pl.when(pl.program_id(0) == 0)
    def _():
        inverse[...] = inverse_factor(gram_one[...] + gram_two[...]).astype(jnp.bfloat16)

    for i in range(0, applied.shape[0], 2):
        pair = jnp.concatenate([applied[i], applied[i + 1]], axis=1)
        value = jnp.dot(inverse[...], pair, preferred_element_type=jnp.float32)
        new[i] = value[:, :BLK].astype(jnp.bfloat16)
        new[i + 1] = value[:, BLK:].astype(jnp.bfloat16)


def new_modes(gram_one, gram_two, applied, steps=3):
    half, modes, _ = applied.shape
    part_spec = pl.BlockSpec((half // steps, modes, BLK), lambda i: (i, 0, 0))
    square_spec = pl.BlockSpec((modes, modes), lambda i: (0, 0))
    return pl.pallas_call(
        solve_kernel,
        out_shape=jax.ShapeDtypeStruct(applied.shape, jnp.bfloat16),
        grid=(steps,),
        in_specs=[square_spec, square_spec, part_spec],
        out_specs=part_spec,
        scratch_shapes=[pltpu.VMEM((modes, modes), jnp.bfloat16)],
        compiler_params=pltpu.CompilerParams(vmem_limit_bytes=VMEM_LIMIT),
    )(gram_one, gram_two, applied)


def side(xh, xl):
    return 1 - (xh ^ xl)


def flat(ny, nz, y, z, c, xh, xl):
    return (((y * nz + z) * 2 + c) * 2 + xh) * 2 + xl


def every(ny, nz):
    return [
        (y, z, c, xh, xl)
        for y in range(ny)
        for z in range(nz)
        for c in range(2)
        for xh in range(2)
        for xl in range(2)
    ]


def next_pairs(ny, nz):
    pairs = []
    for y, z, c, xh, xl in every(ny, nz):
        sub = ((y * nz + z) * 2 + side(xh, xl) + 1) % (ny * nz * 2)
        there = (sub // (2 * nz), sub // 2 % nz, c, xh, xh ^ (1 - sub % 2))
        pairs.append((flat(ny, nz, y, z, c, xh, xl), flat(ny, nz, *there)))
    return pairs


def out_pairs(ny, nz):
    pairs = []
    for y, z, c, xh, xl in every(ny, nz):
        if c != side(xh, xl):
            there = (y, z, 1 - c, xh, 1 - xl)
            pairs.append((flat(ny, nz, y, z, c, xh, xl), flat(ny, nz, *there)))
    return pairs


def spread_pairs():
    return [
        (side(xh, xl) * 4 + xh * 2 + xl, (1 - side(xh, xl)) * 4 + xh * 2 + xl)
        for xh in range(2)
        for xl in range(2)
    ]


def core_swap(value):
    return lax.ppermute(value, "c", [(0, 1), (1, 0)])


def chip_swap(value):
    return lax.ppermute(value, ("xh", "xl"), [(0, 3), (3, 0), (1, 2), (2, 1)])


def slot_rows(targets, wanted, rows):
    equal = targets[..., None, :] == wanted[:, None]
    at = jnp.arange(rows, dtype=jnp.int32)
    first = jnp.min(jnp.where(equal, at, rows), axis=-1)
    last = jnp.max(jnp.where(equal, at, -1), axis=-1)
    valid = jnp.stack([first < rows, last > first], axis=-1)
    return jnp.where(valid, jnp.stack([first, last], axis=-1), 0), valid


def shards(ny, nz, blocks, routes, offsets, live, start_modes):
    y, z, c, xh, xl = [lax.axis_index(axis) for axis in AXES]
    chip = 2 * xh + xl
    own_side = 1 - (xh ^ xl)
    subs = ny * nz * 2
    rows = blocks.shape[0]
    domain, share = start_modes.shape[1], start_modes.shape[2]
    half = domain // 2
    group = ("y", "z", "xl")

    targets = routes[:, 0]
    wanted = jnp.arange(subs, dtype=jnp.int32) ^ (1 - xh)
    order, _ = slot_rows(targets, wanted, rows)
    packed = pack(blocks, order.reshape(-1))
    received = lax.all_to_all(packed, group, split_axis=0, concat_axis=0, tiled=True)

    table = jnp.stack([targets, offsets[:, 0], offsets[:, 1], live], axis=0)
    tables = lax.all_gather(table, group, axis=0, tiled=False)
    here = ((y * nz + z) * 2 + own_side).astype(jnp.int32)
    index, valid = slot_rows(tables[:, 0, :], here[None], rows)
    index, valid = index[:, 0], valid[:, 0]
    onehot = index[..., None] == jnp.arange(rows, dtype=jnp.int32)
    picked = [
        jnp.sum(jnp.where(onehot & valid[..., None], tables[:, None, k, :], 0), axis=-1)
        for k in (1, 2, 3)
    ]
    offs = jnp.stack(picked[:2], axis=-1).reshape(-1)
    alive = picked[2].reshape(-1)

    gathered = lax.all_gather(start_modes[0], ("xh", "xl"), axis=1, tiled=True)
    sibling = lax.ppermute(gathered, ("c", "xh", "xl"), spread_pairs())
    start = jnp.where(c == own_side, gathered, sibling)
    own = lax.dynamic_slice_in_dim(start, c * half, half, 0)
    peer = lax.dynamic_slice_in_dim(start, (1 - c) * half, half, 0)

    sums = column_sums(received, offs, alive, domain)
    sums = sums + core_swap(sums)
    sums = sums + chip_swap(sums)
    forward = next_pairs(ny, nz)
    backward = [(there, here_) for here_, there in forward]
    low = lax.ppermute(sums[domain - OV :], AXES, forward)
    high = lax.ppermute(sums[:OV], AXES, backward)
    column_sq = sums + jnp.concatenate(
        [low, jnp.zeros((domain - 2 * OV, BLK), jnp.float32), high], axis=0
    )
    scale = lax.rsqrt(column_sq + DAMPING)
    damped = lax.dynamic_slice_in_dim(DAMPING * scale * scale, c * half, half, 0)[:, None, :]

    core = c.astype(jnp.int32)[None]
    work = received
    for step in range(ITERS):
        keep, send, *scaled = apply_rows(step == 0, work, offs, alive, core, scale, own, peer)
        if step == 0:
            work = scaled[0]
        other = core_swap(send)
        chip_sum = (keep.astype(jnp.float32) + other.astype(jnp.float32)).astype(jnp.bfloat16)
        last = step == ITERS - 1
        applied, gram, *ritz = form_image(last, chip_sum, chip_swap(chip_sum), own, damped)
        own = new_modes(gram, core_swap(gram), applied)
        if not last:
            peer = core_swap(own)

    ritz = ritz[0] + core_swap(ritz[0])
    at_home = c == own_side
    mine = lax.dynamic_slice_in_dim(own, chip * share, share, 1)
    beside = lax.dynamic_slice_in_dim(own, (chip ^ 1) * share, share, 1)
    held = jnp.where(at_home, mine, beside)
    swapped = core_swap(jnp.where(at_home, beside, mine))
    whole = jnp.where(
        c == 0, jnp.concatenate([held, swapped], 0), jnp.concatenate([swapped, held], 0)
    )
    pairs = out_pairs(ny, nz)
    modes = jnp.where(at_home, whole, lax.ppermute(whole, AXES, pairs))
    ritz = jnp.where(at_home, ritz, lax.ppermute(ritz, AXES, pairs))
    return modes[None], ritz[None]


def solution(mesh, ny=4):
    nz = mesh.shape["sub"] // (2 * ny)
    grid = Mesh(mesh.devices.reshape(ny, nz, 2, 2, 2), AXES)
    subs, inner = ("y", "z", "c"), ("xh", "xl")
    return jax.shard_map(
        functools.partial(shards, ny, nz),
        mesh=grid,
        in_specs=(
            P(subs + inner, None, None, None),
            P(subs + inner, None),
            P(subs + inner, None),
            P(subs + inner),
            P(subs, None, inner, None),
        ),
        out_specs=(P(subs, None, inner, None), P(subs, None, None)),
        check_vma=False,
    )
```

```python
import functools

import jax
import jax.numpy as jnp
from jax import lax
from jax.experimental import pallas as pl
from jax.experimental.pallas import tpu as pltpu
from jax.sharding import Mesh
from jax.sharding import PartitionSpec as P

OV = 8
ITERS = 3
BLK = 128
DAMPING = 32.0
AXES = ("y", "z", "c", "xh", "xl")
NT = (((1,), (1,)), ((), ()))
VMEM_LIMIT = 50 * 2**20


def nt_dot(left, right):
    return lax.dot_general(left, right, NT, preferred_element_type=jnp.float32)


def pack_kernel(order, blocks, packed, sems):
    slots = packed.shape[0]

    def copy(slot):
        return pltpu.make_async_copy(blocks.at[order[slot]], packed.at[slot], sems.at[slot])

    def start(slot, carry):
        copy(slot).start()
        return carry

    def wait(slot, carry):
        copy(slot).wait()
        return carry

    lax.fori_loop(0, slots, start, 0)
    lax.fori_loop(0, slots, wait, 0)


def pack(blocks, order):
    slots = order.shape[0]
    return pl.pallas_call(
        pack_kernel,
        out_shape=jax.ShapeDtypeStruct((slots,) + blocks.shape[1:], blocks.dtype),
        grid_spec=pltpu.PrefetchScalarGridSpec(
            num_scalar_prefetch=1,
            grid=(1,),
            in_specs=[pl.BlockSpec(blocks.shape, lambda i, *_: (0, 0, 0, 0))],
            out_specs=pl.BlockSpec(memory_space=pl.ANY),
            scratch_shapes=[pltpu.SemaphoreType.DMA((slots,))],
        ),
        compiler_params=pltpu.CompilerParams(vmem_limit_bytes=VMEM_LIMIT),
    )(order, blocks)


def sums_kernel(group, offs, live, blk, sums):
    step = pl.program_id(0)

    @pl.when(step == 0)
    def _():
        sums[...] = jnp.zeros_like(sums)

    rows = lax.broadcasted_iota(jnp.int32, (BLK, BLK), 0)

    def body(s, carry):
        slot = step * group + s
        keep = rows < live[slot]
        for k in range(2):
            wide = blk[s, k].astype(jnp.float32)
            part = jnp.sum(jnp.where(keep, wide * wide, 0.0), axis=0, keepdims=True)
            at = pl.ds(offs[2 * slot + k], 1)
            sums[at, :] = sums[at, :] + part
        return carry

    lax.fori_loop(0, group, body, 0)


def column_sums(blocks, offs, live, domain):
    slots = blocks.shape[0]
    group = min(16, slots)
    return pl.pallas_call(
        functools.partial(sums_kernel, group),
        out_shape=jax.ShapeDtypeStruct((domain, BLK), jnp.float32),
        grid_spec=pltpu.PrefetchScalarGridSpec(
            num_scalar_prefetch=2,
            grid=(slots // group,),
            in_specs=[pl.BlockSpec((group, 2, BLK, BLK), lambda i, *_: (i, 0, 0, 0))],
            out_specs=pl.BlockSpec((domain, BLK), lambda i, *_: (0, 0)),
        ),
        compiler_params=pltpu.CompilerParams(vmem_limit_bytes=VMEM_LIMIT),
    )(offs, live, blocks)


def apply_kernel(first, group, unroll, offs, live, core, blk, scale, own, peer, *rest):
    if first:
        keep, send, scaled, modes, total, sems = rest
    else:
        keep, send, modes, total, sems = rest
    step = pl.program_id(0)
    half = keep.shape[0]
    mine = core[0] * half
    other = (1 - core[0]) * half

    @pl.when(step == 0)
    def _():
        one = pltpu.make_async_copy(own, modes.at[pl.ds(mine, half)], sems.at[0])
        two = pltpu.make_async_copy(peer, modes.at[pl.ds(other, half)], sems.at[1])
        one.start()
        two.start()

        def clear(i, carry):
            total[pl.ds(2 * i, 2)] = jnp.zeros((2,) + total.shape[1:], jnp.float32)
            return carry

        lax.fori_loop(0, half, clear, 0)
        one.wait()
        two.wait()

    rows = lax.broadcasted_iota(jnp.int32, (BLK, BLK), 0)

    def body(g, carry):
        wide, places = [], []
        for u in range(unroll):
            s = g * unroll + u
            slot = step * group + s
            place = [offs[2 * slot], offs[2 * slot + 1]]
            pair = [blk[s, 0], blk[s, 1]]
            if first:
                alive = rows < live[slot]
                for k in range(2):
                    value = pair[k].astype(jnp.float32) * scale[pl.ds(place[k], 1), :]
                    pair[k] = jnp.where(alive, value, 0.0).astype(jnp.bfloat16)
                    scaled[s, k] = pair[k]
            wide.append(jnp.concatenate(pair, axis=1))
            places.append(place)
        picked = [jnp.concatenate([modes[p], modes[q]], axis=1) for p, q in places]
        projected = [nt_dot(v, a).astype(jnp.bfloat16) for v, a in zip(picked, wide)]
        spread = [
            jnp.dot(v, a, preferred_element_type=jnp.float32) for v, a in zip(projected, wide)
        ]
        for (p, q), value in zip(places, spread):
            total[p] += value[:, :BLK]
            total[q] += value[:, BLK:]
        return carry

    lax.fori_loop(0, group // unroll, body, 0)

    @pl.when(step == pl.num_programs(0) - 1)
    def _():
        def write(i, carry):
            keep[pl.ds(2 * i, 2)] = total[pl.ds(mine + 2 * i, 2)].astype(jnp.bfloat16)
            send[pl.ds(2 * i, 2)] = total[pl.ds(other + 2 * i, 2)].astype(jnp.bfloat16)
            return carry

        lax.fori_loop(0, half // 2, write, 0)


def apply_rows(first, blocks, offs, live, core, scale, own, peer):
    slots = blocks.shape[0]
    half, modes, _ = own.shape
    group = min(16, slots)
    unroll = min(8, group)
    block_spec = pl.BlockSpec((group, 2, BLK, BLK), lambda i, *_: (i, 0, 0, 0))
    half_spec = pl.BlockSpec((half, modes, BLK), lambda i, *_: (0, 0, 0))
    half_shape = jax.ShapeDtypeStruct(own.shape, jnp.bfloat16)
    out_shape, out_specs = [half_shape, half_shape], [half_spec, half_spec]
    if first:
        out_shape.append(jax.ShapeDtypeStruct(blocks.shape, jnp.bfloat16))
        out_specs.append(block_spec)
    return pl.pallas_call(
        functools.partial(apply_kernel, first, group, unroll),
        out_shape=out_shape,
        grid_spec=pltpu.PrefetchScalarGridSpec(
            num_scalar_prefetch=3,
            grid=(slots // group,),
            in_specs=[
                block_spec,
                pl.BlockSpec(scale.shape, lambda i, *_: (0, 0)),
                pl.BlockSpec(memory_space=pl.ANY),
                pl.BlockSpec(memory_space=pl.ANY),
            ],
            out_specs=out_specs,
            scratch_shapes=[
                pltpu.VMEM((2 * half, modes, BLK), jnp.bfloat16),
                pltpu.VMEM((2 * half, modes, BLK), jnp.float32),
                pltpu.SemaphoreType.DMA((2,)),
            ],
        ),
        compiler_params=pltpu.CompilerParams(vmem_limit_bytes=VMEM_LIMIT),
    )(offs, live, core, blocks, scale, own, peer)


def image_kernel(with_ritz, one, two, own, damped, applied, gram, *rest):
    step = pl.program_id(0)
    ritz = rest[0] if with_ritz else None

    @pl.when(step == 0)
    def _():
        gram[...] = jnp.zeros_like(gram)
        if with_ritz:
            ritz[...] = jnp.zeros_like(ritz)

    gram_part = jnp.zeros(gram.shape, jnp.float32)
    ritz_part = jnp.zeros(gram.shape, jnp.float32)
    for i in range(0, one.shape[0], 2):
        values, olds = [], []
        for l in (i, i + 1):
            old = own[l]
            total = one[l].astype(jnp.float32) + two[l].astype(jnp.float32)
            value = (total + damped[l] * old.astype(jnp.float32)).astype(jnp.bfloat16)
            applied[l] = value
            values.append(value)
            olds.append(old)
        value = jnp.concatenate(values, axis=1)
        gram_part += nt_dot(value, value)
        if with_ritz:
            ritz_part += nt_dot(jnp.concatenate(olds, axis=1), value)
    gram[...] += gram_part
    if with_ritz:
        ritz[...] += ritz_part


def form_image(with_ritz, one, two, own, damped, steps=3):
    half, modes, _ = own.shape
    part = half // steps
    part_spec = pl.BlockSpec((part, modes, BLK), lambda i: (i, 0, 0))
    square_spec = pl.BlockSpec((modes, modes), lambda i: (0, 0))
    square_shape = jax.ShapeDtypeStruct((modes, modes), jnp.float32)
    squares = 2 if with_ritz else 1
    return pl.pallas_call(
        functools.partial(image_kernel, with_ritz),
        out_shape=[jax.ShapeDtypeStruct(own.shape, jnp.bfloat16)] + [square_shape] * squares,
        grid=(steps,),
        in_specs=[part_spec] * 3 + [pl.BlockSpec((part, 1, BLK), lambda i: (i, 0, 0))],
        out_specs=[part_spec] + [square_spec] * squares,
        compiler_params=pltpu.CompilerParams(vmem_limit_bytes=VMEM_LIMIT),
    )(one, two, own, damped)


def inverse_factor(gram):
    size = gram.shape[0]
    both = (size, 2 * size)
    row_at = lax.broadcasted_iota(jnp.int32, both, 0)
    col_at = lax.broadcasted_iota(jnp.int32, both, 1)
    eye = (col_at == row_at + size).astype(jnp.float32)
    work = jnp.where(col_at < size, jnp.concatenate([gram, gram], axis=1), eye)
    for j in range(size):
        root = lax.rsqrt(work[j : j + 1, j : j + 1])
        row = work[j : j + 1, :] * root
        factor = jnp.where(row_at[:, :1] > j, work[:, j : j + 1] * root, 0.0)
        work = jnp.where(row_at == j, row, work - factor * row)
    return work[:, size:]


def solve_kernel(gram_one, gram_two, applied, new, inverse):
    @pl.when(pl.program_id(0) == 0)
    def _():
        inverse[...] = inverse_factor(gram_one[...] + gram_two[...]).astype(jnp.bfloat16)

    for i in range(0, applied.shape[0], 2):
        pair = jnp.concatenate([applied[i], applied[i + 1]], axis=1)
        value = jnp.dot(inverse[...], pair, preferred_element_type=jnp.float32)
        new[i] = value[:, :BLK].astype(jnp.bfloat16)
        new[i + 1] = value[:, BLK:].astype(jnp.bfloat16)


def new_modes(gram_one, gram_two, applied, steps=3):
    half, modes, _ = applied.shape
    part_spec = pl.BlockSpec((half // steps, modes, BLK), lambda i: (i, 0, 0))
    square_spec = pl.BlockSpec((modes, modes), lambda i: (0, 0))
    return pl.pallas_call(
        solve_kernel,
        out_shape=jax.ShapeDtypeStruct(applied.shape, jnp.bfloat16),
        grid=(steps,),
        in_specs=[square_spec, square_spec, part_spec],
        out_specs=part_spec,
        scratch_shapes=[pltpu.VMEM((modes, modes), jnp.bfloat16)],
        compiler_params=pltpu.CompilerParams(vmem_limit_bytes=VMEM_LIMIT),
    )(gram_one, gram_two, applied)


def side(xh, xl):
    return 1 - (xh ^ xl)


def flat(ny, nz, y, z, c, xh, xl):
    return (((y * nz + z) * 2 + c) * 2 + xh) * 2 + xl


def every(ny, nz):
    return [
        (y, z, c, xh, xl)
        for y in range(ny)
        for z in range(nz)
        for c in range(2)
        for xh in range(2)
        for xl in range(2)
    ]


def next_pairs(ny, nz):
    pairs = []
    for y, z, c, xh, xl in every(ny, nz):
        sub = ((y * nz + z) * 2 + side(xh, xl) + 1) % (ny * nz * 2)
        there = (sub // (2 * nz), sub // 2 % nz, c, xh, xh ^ (1 - sub % 2))
        pairs.append((flat(ny, nz, y, z, c, xh, xl), flat(ny, nz, *there)))
    return pairs


def out_pairs(ny, nz):
    pairs = []
    for y, z, c, xh, xl in every(ny, nz):
        if c != side(xh, xl):
            there = (y, z, 1 - c, xh, 1 - xl)
            pairs.append((flat(ny, nz, y, z, c, xh, xl), flat(ny, nz, *there)))
    return pairs


def spread_pairs():
    return [
        (side(xh, xl) * 4 + xh * 2 + xl, (1 - side(xh, xl)) * 4 + xh * 2 + xl)
        for xh in range(2)
        for xl in range(2)
    ]


def core_swap(value):
    return lax.ppermute(value, "c", [(0, 1), (1, 0)])


def chip_swap(value):
    return lax.ppermute(value, ("xh", "xl"), [(0, 3), (3, 0), (1, 2), (2, 1)])


def slot_rows(targets, wanted, rows):
    equal = targets[..., None, :] == wanted[:, None]
    at = jnp.arange(rows, dtype=jnp.int32)
    first = jnp.min(jnp.where(equal, at, rows), axis=-1)
    last = jnp.max(jnp.where(equal, at, -1), axis=-1)
    valid = jnp.stack([first < rows, last > first], axis=-1)
    return jnp.where(valid, jnp.stack([first, last], axis=-1), 0), valid


def shards(ny, nz, blocks, routes, offsets, live, start_modes):
    y, z, c, xh, xl = [lax.axis_index(axis) for axis in AXES]
    chip = 2 * xh + xl
    own_side = 1 - (xh ^ xl)
    subs = ny * nz * 2
    rows = blocks.shape[0]
    domain, share = start_modes.shape[1], start_modes.shape[2]
    half = domain // 2
    group = ("y", "z", "xl")

    targets = routes[:, 0]
    wanted = jnp.arange(subs, dtype=jnp.int32) ^ (1 - xh)
    order, _ = slot_rows(targets, wanted, rows)
    packed = pack(blocks, order.reshape(-1))
    received = lax.all_to_all(packed, group, split_axis=0, concat_axis=0, tiled=True)

    table = jnp.stack([targets, offsets[:, 0], offsets[:, 1], live], axis=0)
    tables = lax.all_gather(table.astype(jnp.float32), AXES, axis=0, tiled=False)
    tables = tables.astype(jnp.int32).reshape(ny, nz, 2, 2, 2, 4, rows)
    tables = lax.dynamic_index_in_dim(tables, c, 2, keepdims=False)
    tables = lax.dynamic_index_in_dim(tables, xh, 2, keepdims=False).reshape(subs, 4, rows)
    here = ((y * nz + z) * 2 + own_side).astype(jnp.int32)
    index, valid = slot_rows(tables[:, 0, :], here[None], rows)
    index, valid = index[:, 0], valid[:, 0]
    onehot = index[..., None] == jnp.arange(rows, dtype=jnp.int32)
    picked = [
        jnp.sum(jnp.where(onehot & valid[..., None], tables[:, None, k, :], 0), axis=-1)
        for k in (1, 2, 3)
    ]
    offs = jnp.stack(picked[:2], axis=-1).reshape(-1)
    alive = picked[2].reshape(-1)

    gathered = lax.all_gather(start_modes[0], ("xh", "xl"), axis=1, tiled=True)
    sibling = lax.ppermute(gathered, ("c", "xh", "xl"), spread_pairs())
    start = jnp.where(c == own_side, gathered, sibling)
    own = lax.dynamic_slice_in_dim(start, c * half, half, 0)
    peer = lax.dynamic_slice_in_dim(start, (1 - c) * half, half, 0)

    sums = column_sums(received, offs, alive, domain)
    sums = sums + core_swap(sums)
    sums = sums + chip_swap(sums)
    forward = next_pairs(ny, nz)
    backward = [(there, here_) for here_, there in forward]
    low = lax.ppermute(sums[domain - OV :], AXES, forward)
    high = lax.ppermute(sums[:OV], AXES, backward)
    column_sq = sums + jnp.concatenate(
        [low, jnp.zeros((domain - 2 * OV, BLK), jnp.float32), high], axis=0
    )
    scale = lax.rsqrt(column_sq + DAMPING)
    damped = lax.dynamic_slice_in_dim(DAMPING * scale * scale, c * half, half, 0)[:, None, :]

    core = c.astype(jnp.int32)[None]
    work = received
    for step in range(ITERS):
        keep, send, *scaled = apply_rows(step == 0, work, offs, alive, core, scale, own, peer)
        if step == 0:
            work = scaled[0]
        other = core_swap(send)
        chip_sum = (keep.astype(jnp.float32) + other.astype(jnp.float32)).astype(jnp.bfloat16)
        last = step == ITERS - 1
        applied, gram, *ritz = form_image(last, chip_sum, chip_swap(chip_sum), own, damped)
        own = new_modes(gram, core_swap(gram), applied)
        if not last:
            peer = core_swap(own)

    ritz = ritz[0] + core_swap(ritz[0])
    at_home = c == own_side
    mine = lax.dynamic_slice_in_dim(own, chip * share, share, 1)
    beside = lax.dynamic_slice_in_dim(own, (chip ^ 1) * share, share, 1)
    held = jnp.where(at_home, mine, beside)
    swapped = core_swap(jnp.where(at_home, beside, mine))
    whole = jnp.where(
        c == 0, jnp.concatenate([held, swapped], 0), jnp.concatenate([swapped, held], 0)
    )
    pairs = out_pairs(ny, nz)
    modes = jnp.where(at_home, whole, lax.ppermute(whole, AXES, pairs))
    ritz = jnp.where(at_home, ritz, lax.ppermute(ritz, AXES, pairs))
    return modes[None], ritz[None]


def solution(mesh, ny=4):
    nz = mesh.shape["sub"] // (2 * ny)
    grid = Mesh(mesh.devices.reshape(ny, nz, 2, 2, 2), AXES)
    subs, inner = ("y", "z", "c"), ("xh", "xl")
    return jax.shard_map(
        functools.partial(shards, ny, nz),
        mesh=grid,
        in_specs=(
            P(subs + inner, None, None, None),
            P(subs + inner, None),
            P(subs + inner, None),
            P(subs + inner),
            P(subs, None, inner, None),
        ),
        out_specs=(P(subs, None, inner, None), P(subs, None, None)),
        check_vma=False,
    )
```

```python
import functools

import jax
import jax.numpy as jnp
from jax import lax
from jax.experimental import pallas as pl
from jax.experimental.pallas import tpu as pltpu
from jax.sharding import Mesh
from jax.sharding import PartitionSpec as P

OV = 8
ITERS = 3
BLK = 128
DAMPING = 32.0
AXES = ("y", "z", "c", "xh", "xl")
NT = (((1,), (1,)), ((), ()))
VMEM_LIMIT = 20 * 2**20
PACK_LIMIT = 50 * 2**20
SMALL_LIMIT = 12 * 2**20


def nt_dot(left, right):
    return lax.dot_general(left, right, NT, preferred_element_type=jnp.float32)


def pack_kernel(order, blocks, packed, sems):
    slots = packed.shape[0]

    def copy(slot):
        return pltpu.make_async_copy(blocks.at[order[slot]], packed.at[slot], sems.at[slot])

    def start(slot, carry):
        copy(slot).start()
        return carry

    def wait(slot, carry):
        copy(slot).wait()
        return carry

    lax.fori_loop(0, slots, start, 0)
    lax.fori_loop(0, slots, wait, 0)


def pack(blocks, order):
    slots = order.shape[0]
    return pl.pallas_call(
        pack_kernel,
        out_shape=jax.ShapeDtypeStruct((slots,) + blocks.shape[1:], blocks.dtype),
        grid_spec=pltpu.PrefetchScalarGridSpec(
            num_scalar_prefetch=1,
            grid=(1,),
            in_specs=[pl.BlockSpec(blocks.shape, lambda i, *_: (0, 0, 0, 0))],
            out_specs=pl.BlockSpec(memory_space=pl.ANY),
            scratch_shapes=[pltpu.SemaphoreType.DMA((slots,))],
        ),
        compiler_params=pltpu.CompilerParams(vmem_limit_bytes=PACK_LIMIT),
    )(order, blocks)


def sums_kernel(group, offs, live, blk, sums):
    step = pl.program_id(0)

    @pl.when(step == 0)
    def _():
        sums[...] = jnp.zeros_like(sums)

    rows = lax.broadcasted_iota(jnp.int32, (BLK, BLK), 0)

    def body(s, carry):
        slot = step * group + s
        keep = rows < live[slot]
        for k in range(2):
            wide = blk[s, k].astype(jnp.float32)
            part = jnp.sum(jnp.where(keep, wide * wide, 0.0), axis=0, keepdims=True)
            at = pl.ds(offs[2 * slot + k], 1)
            sums[at, :] = sums[at, :] + part
        return carry

    lax.fori_loop(0, group, body, 0)


def column_sums(blocks, offs, live, domain):
    slots = blocks.shape[0]
    group = min(16, slots)
    return pl.pallas_call(
        functools.partial(sums_kernel, group),
        out_shape=jax.ShapeDtypeStruct((domain, BLK), jnp.float32),
        grid_spec=pltpu.PrefetchScalarGridSpec(
            num_scalar_prefetch=2,
            grid=(slots // group,),
            in_specs=[pl.BlockSpec((group, 2, BLK, BLK), lambda i, *_: (i, 0, 0, 0))],
            out_specs=pl.BlockSpec((domain, BLK), lambda i, *_: (0, 0)),
        ),
        compiler_params=pltpu.CompilerParams(vmem_limit_bytes=VMEM_LIMIT),
    )(offs, live, blocks)


def apply_kernel(first, group, unroll, offs, live, core, blk, scale, own, peer, *rest):
    if first:
        keep, send, scaled, modes, total, sems = rest
    else:
        keep, send, modes, total, sems = rest
    step = pl.program_id(0)
    half = keep.shape[0]
    mine = core[0] * half
    other = (1 - core[0]) * half

    @pl.when(step == 0)
    def _():
        one = pltpu.make_async_copy(own, modes.at[pl.ds(mine, half)], sems.at[0])
        two = pltpu.make_async_copy(peer, modes.at[pl.ds(other, half)], sems.at[1])
        one.start()
        two.start()

        def clear(i, carry):
            total[pl.ds(2 * i, 2)] = jnp.zeros((2,) + total.shape[1:], jnp.float32)
            return carry

        lax.fori_loop(0, half, clear, 0)
        one.wait()
        two.wait()

    rows = lax.broadcasted_iota(jnp.int32, (BLK, BLK), 0)

    def body(g, carry):
        wide, places = [], []
        for u in range(unroll):
            s = g * unroll + u
            slot = step * group + s
            place = [offs[2 * slot], offs[2 * slot + 1]]
            pair = [blk[s, 0], blk[s, 1]]
            if first:
                alive = rows < live[slot]
                for k in range(2):
                    value = pair[k].astype(jnp.float32) * scale[pl.ds(place[k], 1), :]
                    pair[k] = jnp.where(alive, value, 0.0).astype(jnp.bfloat16)
                    scaled[s, k] = pair[k]
            wide.append(jnp.concatenate(pair, axis=1))
            places.append(place)
        picked = [jnp.concatenate([modes[p], modes[q]], axis=1) for p, q in places]
        projected = [nt_dot(v, a).astype(jnp.bfloat16) for v, a in zip(picked, wide)]
        spread = [
            jnp.dot(v, a, preferred_element_type=jnp.float32) for v, a in zip(projected, wide)
        ]
        for (p, q), value in zip(places, spread):
            total[p] += value[:, :BLK]
            total[q] += value[:, BLK:]
        return carry

    lax.fori_loop(0, group // unroll, body, 0)

    @pl.when(step == pl.num_programs(0) - 1)
    def _():
        def write(i, carry):
            keep[pl.ds(2 * i, 2)] = total[pl.ds(mine + 2 * i, 2)].astype(jnp.bfloat16)
            send[pl.ds(2 * i, 2)] = total[pl.ds(other + 2 * i, 2)].astype(jnp.bfloat16)
            return carry

        lax.fori_loop(0, half // 2, write, 0)


def apply_rows(first, blocks, offs, live, core, scale, own, peer):
    slots = blocks.shape[0]
    half, modes, _ = own.shape
    group = min(16, slots)
    unroll = min(8, group)
    block_spec = pl.BlockSpec((group, 2, BLK, BLK), lambda i, *_: (i, 0, 0, 0))
    half_spec = pl.BlockSpec((half, modes, BLK), lambda i, *_: (0, 0, 0))
    half_shape = jax.ShapeDtypeStruct(own.shape, jnp.bfloat16)
    out_shape, out_specs = [half_shape, half_shape], [half_spec, half_spec]
    if first:
        out_shape.append(jax.ShapeDtypeStruct(blocks.shape, jnp.bfloat16))
        out_specs.append(block_spec)
    return pl.pallas_call(
        functools.partial(apply_kernel, first, group, unroll),
        out_shape=out_shape,
        grid_spec=pltpu.PrefetchScalarGridSpec(
            num_scalar_prefetch=3,
            grid=(slots // group,),
            in_specs=[
                block_spec,
                pl.BlockSpec(scale.shape, lambda i, *_: (0, 0)),
                pl.BlockSpec(memory_space=pl.ANY),
                pl.BlockSpec(memory_space=pl.ANY),
            ],
            out_specs=out_specs,
            scratch_shapes=[
                pltpu.VMEM((2 * half, modes, BLK), jnp.bfloat16),
                pltpu.VMEM((2 * half, modes, BLK), jnp.float32),
                pltpu.SemaphoreType.DMA((2,)),
            ],
        ),
        compiler_params=pltpu.CompilerParams(vmem_limit_bytes=VMEM_LIMIT),
        cost_estimate=pl.CostEstimate(
            flops=10**10, bytes_accessed=12 * 10**6, transcendentals=0
        ),
    )(offs, live, core, blocks, scale, own, peer)


def image_kernel(second, with_ritz, *refs):
    one, two, own, damped, *rest = refs
    before = rest.pop(0) if second else None
    own_before = rest.pop(0) if with_ritz else None
    applied, gram = rest[:2]
    ritz = rest[2] if with_ritz else None

    @pl.when(pl.program_id(0) == 0)
    def _():
        gram[...] = jnp.zeros_like(gram)
        if with_ritz:
            ritz[...] = jnp.zeros_like(ritz)

    gram_part = jnp.zeros(gram.shape, jnp.float32)
    ritz_part = jnp.zeros(ritz.shape, jnp.float32) if with_ritz else None
    for i in range(0, one.shape[0], 2):
        values = []
        for l in (i, i + 1):
            total = one[l].astype(jnp.float32) + two[l].astype(jnp.float32)
            old = own[l].astype(jnp.float32)
            value = (total + damped[l] * old).astype(jnp.bfloat16)
            applied[l] = value
            values.append(value)
        value = jnp.concatenate(values, axis=1)
        everything = value
        if second:
            earlier = jnp.concatenate([before[i], before[i + 1]], axis=1)
            everything = jnp.concatenate([earlier, value], axis=0)
        gram_part += nt_dot(value, everything)
        if with_ritz:
            olds = [jnp.concatenate([own_before[l], own[l]], axis=0) for l in (i, i + 1)]
            ritz_part += nt_dot(jnp.concatenate(olds, axis=1), everything)
    gram[...] += gram_part
    if with_ritz:
        ritz[...] += ritz_part


def form_image(one, two, own, damped, before=(), with_ritz=False, steps=3):
    half, modes, _ = own.shape
    part = half // steps
    second = len(before) > 0
    part_spec = pl.BlockSpec((part, modes, BLK), lambda i: (i, 0, 0))
    shapes = [(modes, 2 * modes if second else modes)] + [(2 * modes, 2 * modes)] * with_ritz
    return pl.pallas_call(
        functools.partial(image_kernel, second, with_ritz),
        out_shape=[jax.ShapeDtypeStruct(own.shape, jnp.bfloat16)]
        + [jax.ShapeDtypeStruct(shape, jnp.float32) for shape in shapes],
        grid=(steps,),
        in_specs=[part_spec] * 3
        + [pl.BlockSpec((part, 1, BLK), lambda i: (i, 0, 0))]
        + [part_spec] * len(before),
        out_specs=[part_spec] + [pl.BlockSpec(shape, lambda i: (0, 0)) for shape in shapes],
        compiler_params=pltpu.CompilerParams(vmem_limit_bytes=SMALL_LIMIT),
        cost_estimate=pl.CostEstimate(flops=10**9, bytes_accessed=4 * 10**6, transcendentals=0),
    )(one, two, own, damped, *before)


def exact(left, right, dims):
    return lax.dot_general(
        left, right, (dims, ((), ())), precision=lax.Precision.HIGHEST,
        preferred_element_type=jnp.float32,
    )


def eliminate(work, size, at):
    row_at = lax.broadcasted_iota(jnp.int32, work.shape, 0)
    for j in range(size):
        root = lax.rsqrt(work[j : j + 1, at + j : at + j + 1])
        row = work[j : j + 1, :] * root
        factor = jnp.where(row_at[:, :1] > j, work[:, at + j : at + j + 1] * root, 0.0)
        work = jnp.where(row_at == j, row, work - factor * row)
    return work


def unit(size):
    at = lax.broadcasted_iota(jnp.int32, (size, size), 0)
    return (at == lax.broadcasted_iota(jnp.int32, (size, size), 1)).astype(jnp.float32)


def first_inverse(gram):
    size = gram.shape[0]
    none = jnp.zeros((size, size), jnp.float32)
    work = jnp.concatenate([unit(size), none, gram, none], axis=1)
    return eliminate(work, size, 2 * size)[:, :size]


def second_inverse(gram, first):
    size = first.shape[0]
    cross = exact(gram[:, :size], first, ((1,), (1,)))
    rest = gram[:, size:] - exact(cross, cross, ((1,), (1,)))
    left = -exact(cross, first, ((1,), (0,)))
    none = jnp.zeros((size, size), jnp.float32)
    work = jnp.concatenate([left, unit(size), rest, none], axis=1)
    return eliminate(work, size, 2 * size)[:, : 2 * size]


def first_kernel(gram_one, gram_two, applied, new, first, inverse):
    @pl.when(pl.program_id(0) == 0)
    def _():
        value = first_inverse(gram_one[...] + gram_two[...])
        first[...] = value
        inverse[...] = value.astype(jnp.bfloat16)

    for i in range(0, applied.shape[0], 2):
        pair = jnp.concatenate([applied[i], applied[i + 1]], axis=1)
        value = jnp.dot(inverse[...], pair, preferred_element_type=jnp.float32)
        new[i] = value[:, :BLK].astype(jnp.bfloat16)
        new[i + 1] = value[:, BLK:].astype(jnp.bfloat16)


def second_kernel(upper, gram_one, gram_two, first, before, applied, new, inverse):
    @pl.when(pl.program_id(0) == 0)
    def _():
        value = second_inverse(gram_one[...] + gram_two[...], first[...])
        above = jnp.concatenate([first[...], jnp.zeros_like(first)], axis=1)
        inverse[...] = jnp.where(upper[0] == 1, above, value).astype(jnp.bfloat16)

    for i in range(0, applied.shape[0], 2):
        both = [jnp.concatenate([before[l], applied[l]], axis=0) for l in (i, i + 1)]
        pair = jnp.concatenate(both, axis=1)
        value = jnp.dot(inverse[...], pair, preferred_element_type=jnp.float32)
        new[i] = value[:, :BLK].astype(jnp.bfloat16)
        new[i + 1] = value[:, BLK:].astype(jnp.bfloat16)


def first_modes(gram_one, gram_two, applied, steps=3):
    half, modes, _ = applied.shape
    part_spec = pl.BlockSpec((half // steps, modes, BLK), lambda i: (i, 0, 0))
    square_spec = pl.BlockSpec((modes, modes), lambda i: (0, 0))
    return pl.pallas_call(
        first_kernel,
        out_shape=[
            jax.ShapeDtypeStruct(applied.shape, jnp.bfloat16),
            jax.ShapeDtypeStruct((modes, modes), jnp.float32),
        ],
        grid=(steps,),
        in_specs=[square_spec, square_spec, part_spec],
        out_specs=[part_spec, square_spec],
        scratch_shapes=[pltpu.VMEM((modes, modes), jnp.bfloat16)],
        compiler_params=pltpu.CompilerParams(vmem_limit_bytes=SMALL_LIMIT),
        cost_estimate=pl.CostEstimate(flops=3 * 10**9, bytes_accessed=10**6, transcendentals=0),
    )(gram_one, gram_two, applied)


def second_modes(upper, gram_one, gram_two, first, before, applied, steps=3):
    half, modes, _ = applied.shape
    part_spec = pl.BlockSpec((half // steps, modes, BLK), lambda i, *_: (i, 0, 0))
    rows_spec = pl.BlockSpec((modes, 2 * modes), lambda i, *_: (0, 0))
    square_spec = pl.BlockSpec((modes, modes), lambda i, *_: (0, 0))
    return pl.pallas_call(
        second_kernel,
        out_shape=jax.ShapeDtypeStruct(applied.shape, jnp.bfloat16),
        grid_spec=pltpu.PrefetchScalarGridSpec(
            num_scalar_prefetch=1,
            grid=(steps,),
            in_specs=[rows_spec, rows_spec, square_spec, part_spec, part_spec],
            out_specs=part_spec,
            scratch_shapes=[pltpu.VMEM((modes, 2 * modes), jnp.bfloat16)],
        ),
        compiler_params=pltpu.CompilerParams(vmem_limit_bytes=SMALL_LIMIT),
        cost_estimate=pl.CostEstimate(flops=3 * 10**9, bytes_accessed=10**6, transcendentals=0),
    )(upper, gram_one, gram_two, first, before, applied)


def side(xh, xl):
    return 1 - (xh ^ xl)


def flat(ny, nz, y, z, c, xh, xl):
    return (((y * nz + z) * 2 + c) * 2 + xh) * 2 + xl


def every(ny, nz):
    return [
        (y, z, c, xh, xl)
        for y in range(ny)
        for z in range(nz)
        for c in range(2)
        for xh in range(2)
        for xl in range(2)
    ]


def next_pairs(ny, nz, cross):
    pairs = []
    for y, z, c, xh, xl in every(ny, nz):
        sub = ((y * nz + z) * 2 + side(xh, xl) + 1) % (ny * nz * 2)
        to = xh ^ cross
        there = (sub // (2 * nz), sub // 2 % nz, c, to, to ^ (1 - sub % 2))
        pairs.append((flat(ny, nz, y, z, c, xh, xl), flat(ny, nz, *there)))
    return pairs


def out_pairs(ny, nz):
    pairs = []
    for y, z, c, xh, xl in every(ny, nz):
        if c != side(xh, xl):
            there = (y, z, 1 - c, xh, 1 - xl)
            pairs.append((flat(ny, nz, y, z, c, xh, xl), flat(ny, nz, *there)))
    return pairs


def spread_pairs():
    return [
        (side(xh, xl) * 4 + xh * 2 + xl, (1 - side(xh, xl)) * 4 + xh * 2 + xl)
        for xh in range(2)
        for xl in range(2)
    ]


def start_pairs(mask):
    return [
        (side(x // 2, x % 2) * 4 + (x ^ mask), side(x // 2, x % 2) * 4 + x) for x in range(4)
    ]


def core_swap(value):
    return lax.ppermute(value, "c", [(0, 1), (1, 0)])


def chip_swap(value):
    return lax.ppermute(value, ("xh", "xl"), [(0, 3), (3, 0), (1, 2), (2, 1)])


def slot_rows(targets, wanted, rows):
    equal = targets[..., None, :] == wanted[:, None]
    at = jnp.arange(rows, dtype=jnp.int32)
    first = jnp.min(jnp.where(equal, at, rows), axis=-1)
    last = jnp.max(jnp.where(equal, at, -1), axis=-1)
    valid = jnp.stack([first < rows, last > first], axis=-1)
    return jnp.where(valid, jnp.stack([first, last], axis=-1), 0), valid


def shards(ny, nz, blocks, routes, offsets, live, start_modes):
    y, z, c, xh, xl = [lax.axis_index(axis) for axis in AXES]
    own_side = 1 - (xh ^ xl)
    subs = ny * nz * 2
    rows = blocks.shape[0]
    domain, share = start_modes.shape[1], start_modes.shape[2]
    half = domain // 2
    group = ("y", "z", "xl")

    targets = routes[:, 0]
    wanted = jnp.arange(subs, dtype=jnp.int32) ^ (1 - xh)
    order, _ = slot_rows(targets, wanted, rows)
    table = jnp.stack([targets, offsets[:, 0], offsets[:, 1], live], axis=0)
    table = jnp.pad(table.astype(jnp.float32), ((0, 4), (0, BLK - rows)))
    packed, table, start_modes = lax.optimization_barrier(
        (pack(blocks, order.reshape(-1)), table, start_modes)
    )
    received = lax.all_to_all(packed, group, split_axis=0, concat_axis=0, tiled=True)

    tables = lax.all_gather(table, AXES, axis=0, tiled=False)[:, :4, :rows]
    tables = tables.astype(jnp.int32).reshape(ny, nz, 2, 2, 2, 4, rows)
    tables = lax.dynamic_index_in_dim(tables, c, 2, keepdims=False)
    tables = lax.dynamic_index_in_dim(tables, xh, 2, keepdims=False).reshape(subs, 4, rows)
    here = ((y * nz + z) * 2 + own_side).astype(jnp.int32)
    index, valid = slot_rows(tables[:, 0, :], here[None], rows)
    index, valid = index[:, 0], valid[:, 0]
    onehot = index[..., None] == jnp.arange(rows, dtype=jnp.int32)
    picked = [
        jnp.sum(jnp.where(onehot & valid[..., None], tables[:, None, k, :], 0), axis=-1)
        for k in (1, 2, 3)
    ]
    offs = jnp.stack(picked[:2], axis=-1).reshape(-1)
    alive = picked[2].reshape(-1)

    by = [start_modes[0]] + [
        lax.ppermute(start_modes[0], ("c", "xh", "xl"), start_pairs(mask)) for mask in (1, 2, 3)
    ]
    quarters = []
    for q in range(4):
        near = [jnp.where(xl == q % 2, by[2 * m], by[2 * m + 1]) for m in range(2)]
        quarters.append(jnp.where(xh == q // 2, near[0], near[1]))
    gathered = jnp.concatenate(quarters, axis=1)
    sibling = lax.ppermute(gathered, ("c", "xh", "xl"), spread_pairs())
    start = jnp.where(c == own_side, gathered, sibling)
    cut = start.shape[1] // 2
    owns, peers = [
        [
            lax.dynamic_slice(start, (at * half, h * cut, 0), (half, cut, BLK))
            for h in range(2)
        ]
        for at in (c, 1 - c)
    ]

    sums = column_sums(received, offs, alive, domain)
    sums = sums + core_swap(sums)
    low, high = [], []
    for cross in range(2):
        forward = next_pairs(ny, nz, cross)
        backward = [(there, here_) for here_, there in forward]
        low.append(lax.ppermute(sums[domain - OV :], AXES, forward))
        high.append(lax.ppermute(sums[:OV], AXES, backward))
    column_sq = (sums + chip_swap(sums)) + jnp.concatenate(
        [low[0] + low[1], jnp.zeros((domain - 2 * OV, BLK), jnp.float32), high[0] + high[1]],
        axis=0,
    )
    scale = lax.rsqrt(column_sq + DAMPING)
    damped = lax.dynamic_slice_in_dim(DAMPING * scale * scale, c * half, half, 0)[:, None, :]

    core = c.astype(jnp.int32)[None]
    def apply_half(h, first=False):
        return apply_rows(first, work, offs, alive, core, scale, owns[h], peers[h])

    def add_cores(keep, send, after=None):
        other = core_swap(send)
        if after is not None:
            keep, _ = lax.optimization_barrier((keep, after))
        return (keep.astype(jnp.float32) + other.astype(jnp.float32)).astype(jnp.bfloat16)

    work = received
    lower = jnp.zeros((1,), jnp.int32)
    keep, send, work = apply_half(0, True)
    one = add_cores(keep, send)
    one, owns[1] = lax.optimization_barrier((one, owns[1]))
    for step in range(ITERS):
        last = step == ITERS - 1
        one_there = chip_swap(one)
        two = apply_half(1)
        before, gram = form_image(one, one_there, owns[0], damped)
        two = add_cores(*two, after=gram)
        two_there = chip_swap(two)
        new, first = first_modes(gram, core_swap(gram), before)
        if last:
            two_there, first = lax.optimization_barrier((two_there, first))
            applied, gram, ritz = form_image(
                two, two_there, owns[1], damped, (before, owns[0]), True
            )
            upper = (1 - xh).astype(jnp.int32)[None]
            out = second_modes(upper, gram, core_swap(gram), first, before, applied)
        else:
            owns[0], peers[0] = new, core_swap(new)
            one = apply_half(0)
            applied, gram = form_image(two, two_there, owns[1], damped, (before,))
            one = add_cores(*one, after=gram)
            new = second_modes(lower, gram, core_swap(gram), first, before, applied)
            owns[1], peers[1] = new, core_swap(new)

    ritz = ritz + core_swap(ritz)
    at_home = c == own_side
    mine = lax.dynamic_slice_in_dim(out, xl * share, share, 1)
    beside = lax.dynamic_slice_in_dim(out, (1 - xl) * share, share, 1)
    held = jnp.where(at_home, mine, beside)
    swapped = core_swap(jnp.where(at_home, beside, mine))
    whole = jnp.where(
        c == 0, jnp.concatenate([held, swapped], 0), jnp.concatenate([swapped, held], 0)
    )
    pairs = out_pairs(ny, nz)
    modes = jnp.where(at_home, whole, lax.ppermute(whole, AXES, pairs))
    ritz = jnp.where(at_home, ritz, lax.ppermute(ritz, AXES, pairs))
    return modes[None], ritz[None]


def solution(mesh, ny=4):
    nz = mesh.shape["sub"] // (2 * ny)
    grid = Mesh(mesh.devices.reshape(ny, nz, 2, 2, 2), AXES)
    subs, inner = ("y", "z", "c"), ("xh", "xl")
    return jax.shard_map(
        functools.partial(shards, ny, nz),
        mesh=grid,
        in_specs=(
            P(subs + inner, None, None, None),
            P(subs + inner, None),
            P(subs + inner, None),
            P(subs + inner),
            P(subs, None, inner, None),
        ),
        out_specs=(P(subs, None, inner, None), P(subs, None, None)),
        check_vma=False,
    )
```

```python
import functools

import jax
import jax.numpy as jnp
from jax import lax
from jax.experimental import pallas as pl
from jax.experimental.pallas import tpu as pltpu
from jax.sharding import Mesh
from jax.sharding import PartitionSpec as P

OV = 8
ITERS = 3
BLK = 128
DAMPING = 32.0
AXES = ("y", "z", "c", "xh", "xl")
NT = (((1,), (1,)), ((), ()))
VMEM_LIMIT = 20 * 2**20
PACK_LIMIT = 50 * 2**20
SMALL_LIMIT = 12 * 2**20


def nt_dot(left, right):
    return lax.dot_general(left, right, NT, preferred_element_type=jnp.float32)


def pack_kernel(order, blocks, packed, sems):
    slots = packed.shape[0]

    def copy(slot):
        return pltpu.make_async_copy(blocks.at[order[slot]], packed.at[slot], sems.at[slot])

    def start(slot, carry):
        copy(slot).start()
        return carry

    def wait(slot, carry):
        copy(slot).wait()
        return carry

    lax.fori_loop(0, slots, start, 0)
    lax.fori_loop(0, slots, wait, 0)


def pack(blocks, order):
    slots = order.shape[0]
    return pl.pallas_call(
        pack_kernel,
        out_shape=jax.ShapeDtypeStruct((slots,) + blocks.shape[1:], blocks.dtype),
        grid_spec=pltpu.PrefetchScalarGridSpec(
            num_scalar_prefetch=1,
            grid=(1,),
            in_specs=[pl.BlockSpec(blocks.shape, lambda i, *_: (0, 0, 0, 0))],
            out_specs=pl.BlockSpec(memory_space=pl.ANY),
            scratch_shapes=[pltpu.SemaphoreType.DMA((slots,))],
        ),
        compiler_params=pltpu.CompilerParams(vmem_limit_bytes=PACK_LIMIT),
    )(order, blocks)


def sums_kernel(group, offs, live, left, right, sums):
    step = pl.program_id(0)

    @pl.when(step == 0)
    def _():
        sums[...] = jnp.zeros_like(sums)

    rows = lax.broadcasted_iota(jnp.int32, (BLK, BLK), 0)

    def body(s, carry):
        slot = step * group + s
        keep = rows < live[slot]
        for k in range(2):
            wide = (left, right)[k][s, 0].astype(jnp.float32)
            part = jnp.sum(jnp.where(keep, wide * wide, 0.0), axis=0, keepdims=True)
            at = pl.ds(offs[2 * slot + k], 1)
            sums[at, :] = sums[at, :] + part
        return carry

    lax.fori_loop(0, group, body, 0)


def column_sums(blocks, offs, live, domain):
    slots = blocks.shape[0]
    group = min(16, slots)
    return pl.pallas_call(
        functools.partial(sums_kernel, group),
        out_shape=jax.ShapeDtypeStruct((domain, BLK), jnp.float32),
        grid_spec=pltpu.PrefetchScalarGridSpec(
            num_scalar_prefetch=2,
            grid=(slots // group,),
            in_specs=[
                pl.BlockSpec((group, 1, BLK, BLK), lambda i, *_: (i, 0, 0, 0)),
                pl.BlockSpec((group, 1, BLK, BLK), lambda i, *_: (i, 1, 0, 0)),
            ],
            out_specs=pl.BlockSpec((domain, BLK), lambda i, *_: (0, 0)),
        ),
        compiler_params=pltpu.CompilerParams(vmem_limit_bytes=VMEM_LIMIT),
    )(offs, live, blocks, blocks)


def apply_kernel(first, group, unroll, offs, live, core, blk, scale, own, peer, *rest):
    if first:
        keep, send, scaled, modes, total, sems = rest
    else:
        keep, send, modes, total, sems = rest
    step = pl.program_id(0)
    half = keep.shape[0]
    mine = core[0] * half
    other = (1 - core[0]) * half

    @pl.when(step == 0)
    def _():
        one = pltpu.make_async_copy(own, modes.at[pl.ds(mine, half)], sems.at[0])
        two = pltpu.make_async_copy(peer, modes.at[pl.ds(other, half)], sems.at[1])
        one.start()
        two.start()

        def clear(i, carry):
            total[pl.ds(2 * i, 2)] = jnp.zeros((2,) + total.shape[1:], jnp.float32)
            return carry

        lax.fori_loop(0, half, clear, 0)
        one.wait()
        two.wait()

    rows = lax.broadcasted_iota(jnp.int32, (BLK, BLK), 0)

    def body(g, carry):
        wide, places = [], []
        for u in range(unroll):
            s = g * unroll + u
            slot = step * group + s
            place = [offs[2 * slot], offs[2 * slot + 1]]
            pair = [blk[s, 0], blk[s, 1]]
            if first:
                alive = rows < live[slot]
                for k in range(2):
                    value = pair[k].astype(jnp.float32) * scale[pl.ds(place[k], 1), :]
                    pair[k] = jnp.where(alive, value, 0.0).astype(jnp.bfloat16)
                    scaled[s, k] = pair[k]
            wide.append(jnp.concatenate(pair, axis=1))
            places.append(place)
        picked = [jnp.concatenate([modes[p], modes[q]], axis=1) for p, q in places]
        projected = [nt_dot(v, a).astype(jnp.bfloat16) for v, a in zip(picked, wide)]
        spread = [
            jnp.dot(v, a, preferred_element_type=jnp.float32) for v, a in zip(projected, wide)
        ]
        for (p, q), value in zip(places, spread):
            total[p] += value[:, :BLK]
            total[q] += value[:, BLK:]
        return carry

    lax.fori_loop(0, group // unroll, body, 0)

    @pl.when(step == pl.num_programs(0) - 1)
    def _():
        def write(i, carry):
            keep[pl.ds(2 * i, 2)] = total[pl.ds(mine + 2 * i, 2)].astype(jnp.bfloat16)
            send[pl.ds(2 * i, 2)] = total[pl.ds(other + 2 * i, 2)].astype(jnp.bfloat16)
            return carry

        lax.fori_loop(0, half // 2, write, 0)


def apply_rows(first, blocks, offs, live, core, scale, own, peer):
    slots = blocks.shape[0]
    half, modes, _ = own.shape
    group = min(16, slots)
    unroll = min(8, group)
    block_spec = pl.BlockSpec((group, 2, BLK, BLK), lambda i, *_: (i, 0, 0, 0))
    half_spec = pl.BlockSpec((half, modes, BLK), lambda i, *_: (0, 0, 0))
    half_shape = jax.ShapeDtypeStruct(own.shape, jnp.bfloat16)
    out_shape, out_specs = [half_shape, half_shape], [half_spec, half_spec]
    if first:
        out_shape.append(jax.ShapeDtypeStruct(blocks.shape, jnp.bfloat16))
        out_specs.append(block_spec)
    return pl.pallas_call(
        functools.partial(apply_kernel, first, group, unroll),
        out_shape=out_shape,
        grid_spec=pltpu.PrefetchScalarGridSpec(
            num_scalar_prefetch=3,
            grid=(slots // group,),
            in_specs=[
                block_spec,
                pl.BlockSpec(scale.shape, lambda i, *_: (0, 0)),
                pl.BlockSpec(memory_space=pl.ANY),
                pl.BlockSpec(memory_space=pl.ANY),
            ],
            out_specs=out_specs,
            scratch_shapes=[
                pltpu.VMEM((2 * half, modes, BLK), jnp.bfloat16),
                pltpu.VMEM((2 * half, modes, BLK), jnp.float32),
                pltpu.SemaphoreType.DMA((2,)),
            ],
        ),
        compiler_params=pltpu.CompilerParams(vmem_limit_bytes=VMEM_LIMIT),
        cost_estimate=pl.CostEstimate(
            flops=10**10, bytes_accessed=12 * 10**6, transcendentals=0
        ),
    )(offs, live, core, blocks, scale, own, peer)


def image_kernel(second, with_ritz, *refs):
    one, two, own, damped, *rest = refs
    before = rest.pop(0) if second else None
    own_before = rest.pop(0) if with_ritz else None
    applied, gram = rest[:2]
    ritz = rest[2] if with_ritz else None

    @pl.when(pl.program_id(0) == 0)
    def _():
        gram[...] = jnp.zeros_like(gram)
        if with_ritz:
            ritz[...] = jnp.zeros_like(ritz)

    gram_part = jnp.zeros(gram.shape, jnp.float32)
    ritz_part = jnp.zeros(ritz.shape, jnp.float32) if with_ritz else None
    for i in range(0, one.shape[0], 2):
        values = []
        for l in (i, i + 1):
            total = one[l].astype(jnp.float32) + two[l].astype(jnp.float32)
            old = own[l].astype(jnp.float32)
            value = (total + damped[l] * old).astype(jnp.bfloat16)
            applied[l] = value
            values.append(value)
        value = jnp.concatenate(values, axis=1)
        everything = value
        if second:
            earlier = jnp.concatenate([before[i], before[i + 1]], axis=1)
            everything = jnp.concatenate([earlier, value], axis=0)
        gram_part += nt_dot(value, everything)
        if with_ritz:
            olds = [jnp.concatenate([own_before[l], own[l]], axis=0) for l in (i, i + 1)]
            ritz_part += nt_dot(jnp.concatenate(olds, axis=1), everything)
    gram[...] += gram_part
    if with_ritz:
        ritz[...] += ritz_part


def form_image(one, two, own, damped, before=(), with_ritz=False, steps=3):
    half, modes, _ = own.shape
    part = half // steps
    second = len(before) > 0
    part_spec = pl.BlockSpec((part, modes, BLK), lambda i: (i, 0, 0))
    shapes = [(modes, 2 * modes if second else modes)] + [(2 * modes, 2 * modes)] * with_ritz
    return pl.pallas_call(
        functools.partial(image_kernel, second, with_ritz),
        out_shape=[jax.ShapeDtypeStruct(own.shape, jnp.bfloat16)]
        + [jax.ShapeDtypeStruct(shape, jnp.float32) for shape in shapes],
        grid=(steps,),
        in_specs=[part_spec] * 3
        + [pl.BlockSpec((part, 1, BLK), lambda i: (i, 0, 0))]
        + [part_spec] * len(before),
        out_specs=[part_spec] + [pl.BlockSpec(shape, lambda i: (0, 0)) for shape in shapes],
        compiler_params=pltpu.CompilerParams(vmem_limit_bytes=SMALL_LIMIT),
        cost_estimate=pl.CostEstimate(flops=10**9, bytes_accessed=4 * 10**6, transcendentals=0),
    )(one, two, own, damped, *before)


def exact(left, right, dims):
    return lax.dot_general(
        left, right, (dims, ((), ())), precision=lax.Precision.HIGHEST,
        preferred_element_type=jnp.float32,
    )


def eliminate(work, size, at):
    row_at = lax.broadcasted_iota(jnp.int32, work.shape, 0)
    for j in range(size):
        root = lax.rsqrt(work[j : j + 1, at + j : at + j + 1])
        row = work[j : j + 1, :] * root
        factor = jnp.where(row_at[:, :1] > j, work[:, at + j : at + j + 1] * root, 0.0)
        work = jnp.where(row_at == j, row, work - factor * row)
    return work


def unit(size):
    at = lax.broadcasted_iota(jnp.int32, (size, size), 0)
    return (at == lax.broadcasted_iota(jnp.int32, (size, size), 1)).astype(jnp.float32)


def first_inverse(gram):
    size = gram.shape[0]
    none = jnp.zeros((size, size), jnp.float32)
    work = jnp.concatenate([unit(size), none, gram, none], axis=1)
    return eliminate(work, size, 2 * size)[:, :size]


def second_inverse(gram, first):
    size = first.shape[0]
    cross = exact(gram[:, :size], first, ((1,), (1,)))
    rest = gram[:, size:] - exact(cross, cross, ((1,), (1,)))
    left = -exact(cross, first, ((1,), (0,)))
    none = jnp.zeros((size, size), jnp.float32)
    work = jnp.concatenate([left, unit(size), rest, none], axis=1)
    return eliminate(work, size, 2 * size)[:, : 2 * size]


def first_kernel(gram_one, gram_two, applied, new, first, inverse):
    @pl.when(pl.program_id(0) == 0)
    def _():
        value = first_inverse(gram_one[...] + gram_two[...])
        first[...] = value
        inverse[...] = value.astype(jnp.bfloat16)

    for i in range(0, applied.shape[0], 2):
        pair = jnp.concatenate([applied[i], applied[i + 1]], axis=1)
        value = jnp.dot(inverse[...], pair, preferred_element_type=jnp.float32)
        new[i] = value[:, :BLK].astype(jnp.bfloat16)
        new[i + 1] = value[:, BLK:].astype(jnp.bfloat16)


def second_kernel(upper, gram_one, gram_two, first, before, applied, new, inverse):
    @pl.when(pl.program_id(0) == 0)
    def _():
        value = second_inverse(gram_one[...] + gram_two[...], first[...])
        above = jnp.concatenate([first[...], jnp.zeros_like(first)], axis=1)
        inverse[...] = jnp.where(upper[0] == 1, above, value).astype(jnp.bfloat16)

    for i in range(0, applied.shape[0], 2):
        both = [jnp.concatenate([before[l], applied[l]], axis=0) for l in (i, i + 1)]
        pair = jnp.concatenate(both, axis=1)
        value = jnp.dot(inverse[...], pair, preferred_element_type=jnp.float32)
        new[i] = value[:, :BLK].astype(jnp.bfloat16)
        new[i + 1] = value[:, BLK:].astype(jnp.bfloat16)


def first_modes(gram_one, gram_two, applied, steps=3):
    half, modes, _ = applied.shape
    part_spec = pl.BlockSpec((half // steps, modes, BLK), lambda i: (i, 0, 0))
    square_spec = pl.BlockSpec((modes, modes), lambda i: (0, 0))
    return pl.pallas_call(
        first_kernel,
        out_shape=[
            jax.ShapeDtypeStruct(applied.shape, jnp.bfloat16),
            jax.ShapeDtypeStruct((modes, modes), jnp.float32),
        ],
        grid=(steps,),
        in_specs=[square_spec, square_spec, part_spec],
        out_specs=[part_spec, square_spec],
        scratch_shapes=[pltpu.VMEM((modes, modes), jnp.bfloat16)],
        compiler_params=pltpu.CompilerParams(vmem_limit_bytes=SMALL_LIMIT),
        cost_estimate=pl.CostEstimate(flops=3 * 10**9, bytes_accessed=10**6, transcendentals=0),
    )(gram_one, gram_two, applied)


def second_modes(upper, gram_one, gram_two, first, before, applied, steps=3):
    half, modes, _ = applied.shape
    part_spec = pl.BlockSpec((half // steps, modes, BLK), lambda i, *_: (i, 0, 0))
    rows_spec = pl.BlockSpec((modes, 2 * modes), lambda i, *_: (0, 0))
    square_spec = pl.BlockSpec((modes, modes), lambda i, *_: (0, 0))
    return pl.pallas_call(
        second_kernel,
        out_shape=jax.ShapeDtypeStruct(applied.shape, jnp.bfloat16),
        grid_spec=pltpu.PrefetchScalarGridSpec(
            num_scalar_prefetch=1,
            grid=(steps,),
            in_specs=[rows_spec, rows_spec, square_spec, part_spec, part_spec],
            out_specs=part_spec,
            scratch_shapes=[pltpu.VMEM((modes, 2 * modes), jnp.bfloat16)],
        ),
        compiler_params=pltpu.CompilerParams(vmem_limit_bytes=SMALL_LIMIT),
        cost_estimate=pl.CostEstimate(flops=3 * 10**9, bytes_accessed=10**6, transcendentals=0),
    )(upper, gram_one, gram_two, first, before, applied)


def side(xh, xl):
    return 1 - (xh ^ xl)


def flat(ny, nz, y, z, c, xh, xl):
    return (((y * nz + z) * 2 + c) * 2 + xh) * 2 + xl


def every(ny, nz):
    return [
        (y, z, c, xh, xl)
        for y in range(ny)
        for z in range(nz)
        for c in range(2)
        for xh in range(2)
        for xl in range(2)
    ]


def next_pairs(ny, nz, cross):
    pairs = []
    for y, z, c, xh, xl in every(ny, nz):
        sub = ((y * nz + z) * 2 + side(xh, xl) + 1) % (ny * nz * 2)
        to = xh ^ cross
        there = (sub // (2 * nz), sub // 2 % nz, c, to, to ^ (1 - sub % 2))
        pairs.append((flat(ny, nz, y, z, c, xh, xl), flat(ny, nz, *there)))
    return pairs


def out_pairs(ny, nz):
    pairs = []
    for y, z, c, xh, xl in every(ny, nz):
        if c != side(xh, xl):
            there = (y, z, 1 - c, xh, 1 - xl)
            pairs.append((flat(ny, nz, y, z, c, xh, xl), flat(ny, nz, *there)))
    return pairs


def spread_pairs():
    return [
        (side(xh, xl) * 4 + xh * 2 + xl, (1 - side(xh, xl)) * 4 + xh * 2 + xl)
        for xh in range(2)
        for xl in range(2)
    ]


def start_pairs(mask):
    return [
        (side(x // 2, x % 2) * 4 + (x ^ mask), side(x // 2, x % 2) * 4 + x) for x in range(4)
    ]


def core_swap(value):
    return lax.ppermute(value, "c", [(0, 1), (1, 0)])


def chip_swap(value):
    return lax.ppermute(value, ("xh", "xl"), [(0, 3), (3, 0), (1, 2), (2, 1)])


def slot_rows(targets, wanted, rows):
    equal = targets[..., None, :] == wanted[:, None]
    at = jnp.arange(rows, dtype=jnp.int32)
    first = jnp.min(jnp.where(equal, at, rows), axis=-1)
    last = jnp.max(jnp.where(equal, at, -1), axis=-1)
    valid = jnp.stack([first < rows, last > first], axis=-1)
    return jnp.where(valid, jnp.stack([first, last], axis=-1), 0), valid


def shards(ny, nz, blocks, routes, offsets, live, start_modes):
    y, z, c, xh, xl = [lax.axis_index(axis) for axis in AXES]
    own_side = 1 - (xh ^ xl)
    subs = ny * nz * 2
    rows = blocks.shape[0]
    domain, share = start_modes.shape[1], start_modes.shape[2]
    half = domain // 2
    group = ("y", "z", "xl")

    targets = routes[:, 0]
    wanted = jnp.arange(subs, dtype=jnp.int32) ^ (1 - xh)
    order, _ = slot_rows(targets, wanted, rows)
    table = jnp.stack([targets, offsets[:, 0], offsets[:, 1], live], axis=0)
    table = jnp.pad(table.astype(jnp.float32), ((0, 4), (0, BLK - rows)))
    packed, table, start_modes = lax.optimization_barrier(
        (pack(blocks, order.reshape(-1)), table, start_modes)
    )
    received = lax.all_to_all(packed, group, split_axis=0, concat_axis=0, tiled=True)

    tables = lax.all_gather(table, AXES, axis=0, tiled=False)[:, :4, :rows]
    tables = tables.astype(jnp.int32).reshape(ny, nz, 2, 2, 2, 4, rows)
    tables = lax.dynamic_index_in_dim(tables, c, 2, keepdims=False)
    tables = lax.dynamic_index_in_dim(tables, xh, 2, keepdims=False).reshape(subs, 4, rows)
    here = ((y * nz + z) * 2 + own_side).astype(jnp.int32)
    index, valid = slot_rows(tables[:, 0, :], here[None], rows)
    index, valid = index[:, 0], valid[:, 0]
    onehot = index[..., None] == jnp.arange(rows, dtype=jnp.int32)
    picked = [
        jnp.sum(jnp.where(onehot & valid[..., None], tables[:, None, k, :], 0), axis=-1)
        for k in (1, 2, 3)
    ]
    offs = jnp.stack(picked[:2], axis=-1).reshape(-1)
    alive = picked[2].reshape(-1)

    by = [start_modes[0]] + [
        lax.ppermute(start_modes[0], ("c", "xh", "xl"), start_pairs(mask)) for mask in (1, 2, 3)
    ]
    quarters = []
    for q in range(4):
        near = [jnp.where(xl == q % 2, by[2 * m], by[2 * m + 1]) for m in range(2)]
        quarters.append(jnp.where(xh == q // 2, near[0], near[1]))
    gathered = jnp.concatenate(quarters, axis=1)
    sibling = lax.ppermute(gathered, ("c", "xh", "xl"), spread_pairs())
    start = jnp.where(c == own_side, gathered, sibling)
    cut = start.shape[1] // 2
    owns, peers = [
        [
            lax.dynamic_slice(start, (at * half, h * cut, 0), (half, cut, BLK))
            for h in range(2)
        ]
        for at in (c, 1 - c)
    ]

    sums = column_sums(received, offs, alive, domain)
    sums = sums + core_swap(sums)
    low, high = [], []
    for cross in range(2):
        forward = next_pairs(ny, nz, cross)
        backward = [(there, here_) for here_, there in forward]
        low.append(lax.ppermute(sums[domain - OV :], AXES, forward))
        high.append(lax.ppermute(sums[:OV], AXES, backward))
    column_sq = (sums + chip_swap(sums)) + jnp.concatenate(
        [low[0] + low[1], jnp.zeros((domain - 2 * OV, BLK), jnp.float32), high[0] + high[1]],
        axis=0,
    )
    scale = lax.rsqrt(column_sq + DAMPING)
    damped = lax.dynamic_slice_in_dim(DAMPING * scale * scale, c * half, half, 0)[:, None, :]

    core = c.astype(jnp.int32)[None]
    def apply_half(h, first=False):
        return apply_rows(first, work, offs, alive, core, scale, owns[h], peers[h])

    def add_cores(keep, send, after=None):
        other = core_swap(send)
        if after is not None:
            keep, _ = lax.optimization_barrier((keep, after))
        return (keep.astype(jnp.float32) + other.astype(jnp.float32)).astype(jnp.bfloat16)

    work = received
    lower = jnp.zeros((1,), jnp.int32)
    keep, send, work = apply_half(0, True)
    one = add_cores(keep, send)
    one, owns[1] = lax.optimization_barrier((one, owns[1]))
    for step in range(ITERS):
        last = step == ITERS - 1
        one_there = chip_swap(one)
        keep, send = apply_half(1)
        one_there, keep = lax.optimization_barrier((one_there, keep))
        before, gram = form_image(one, one_there, owns[0], damped)
        two = add_cores(keep, send, after=gram)
        two_there = chip_swap(two)
        two, gram = lax.optimization_barrier((two, gram))
        new, first = first_modes(gram, core_swap(gram), before)
        if last:
            two_there, first = lax.optimization_barrier((two_there, first))
            applied, gram, ritz = form_image(
                two, two_there, owns[1], damped, (before, owns[0]), True
            )
            upper = (1 - xh).astype(jnp.int32)[None]
            out = second_modes(upper, gram, core_swap(gram), first, before, applied)
        else:
            owns[0], peers[0] = new, core_swap(new)
            keep, send = apply_half(0)
            two_there, keep = lax.optimization_barrier((two_there, keep))
            applied, gram = form_image(two, two_there, owns[1], damped, (before,))
            one = add_cores(keep, send, after=gram)
            one, gram = lax.optimization_barrier((one, gram))
            new = second_modes(lower, gram, core_swap(gram), first, before, applied)
            owns[1], peers[1] = new, core_swap(new)

    ritz = ritz + core_swap(ritz)
    at_home = c == own_side
    mine = lax.dynamic_slice_in_dim(out, xl * share, share, 1)
    beside = lax.dynamic_slice_in_dim(out, (1 - xl) * share, share, 1)
    held = jnp.where(at_home, mine, beside)
    swapped = core_swap(jnp.where(at_home, beside, mine))
    whole = jnp.where(
        c == 0, jnp.concatenate([held, swapped], 0), jnp.concatenate([swapped, held], 0)
    )
    pairs = out_pairs(ny, nz)
    modes = jnp.where(at_home, whole, lax.ppermute(whole, AXES, pairs))
    ritz = jnp.where(at_home, ritz, lax.ppermute(ritz, AXES, pairs))
    return modes[None], ritz[None]


def solution(mesh, ny=4):
    nz = mesh.shape["sub"] // (2 * ny)
    grid = Mesh(mesh.devices.reshape(ny, nz, 2, 2, 2), AXES)
    subs, inner = ("y", "z", "c"), ("xh", "xl")
    return jax.shard_map(
        functools.partial(shards, ny, nz),
        mesh=grid,
        in_specs=(
            P(subs + inner, None, None, None),
            P(subs + inner, None),
            P(subs + inner, None),
            P(subs + inner),
            P(subs, None, inner, None),
        ),
        out_specs=(P(subs, None, inner, None), P(subs, None, None)),
        check_vma=False,
    )
```

```python
import functools

import jax
import jax.numpy as jnp
from jax import lax
from jax.experimental import pallas as pl
from jax.experimental.pallas import tpu as pltpu
from jax.sharding import Mesh
from jax.sharding import PartitionSpec as P

OV = 8
ITERS = 3
BLK = 128
DAMPING = 32.0
AXES = ("y", "z", "c", "xh", "xl")
NT = (((1,), (1,)), ((), ()))
VMEM_LIMIT = 20 * 2**20
PACK_LIMIT = 50 * 2**20
SMALL_LIMIT = 12 * 2**20


def nt_dot(left, right):
    return lax.dot_general(left, right, NT, preferred_element_type=jnp.float32)


def pack_kernel(order, blocks, packed, sems):
    slots = packed.shape[0]

    def copy(slot):
        return pltpu.make_async_copy(blocks.at[order[slot]], packed.at[slot], sems.at[slot])

    def start(slot, carry):
        copy(slot).start()
        return carry

    def wait(slot, carry):
        copy(slot).wait()
        return carry

    lax.fori_loop(0, slots, start, 0)
    lax.fori_loop(0, slots, wait, 0)


def pack(blocks, order):
    slots = order.shape[0]
    return pl.pallas_call(
        pack_kernel,
        out_shape=jax.ShapeDtypeStruct((slots,) + blocks.shape[1:], blocks.dtype),
        grid_spec=pltpu.PrefetchScalarGridSpec(
            num_scalar_prefetch=1,
            grid=(1,),
            in_specs=[pl.BlockSpec(blocks.shape, lambda i, *_: (0, 0, 0, 0))],
            out_specs=pl.BlockSpec(memory_space=pl.ANY),
            scratch_shapes=[pltpu.SemaphoreType.DMA((slots,))],
        ),
        compiler_params=pltpu.CompilerParams(vmem_limit_bytes=PACK_LIMIT),
    )(order, blocks)


def sums_kernel(group, offs, live, left, right, sums):
    step = pl.program_id(0)

    @pl.when(step == 0)
    def _():
        sums[...] = jnp.zeros_like(sums)

    rows = lax.broadcasted_iota(jnp.int32, (BLK, BLK), 0)

    def body(s, carry):
        slot = step * group + s
        keep = rows < live[slot]
        for k in range(2):
            wide = (left, right)[k][s, 0].astype(jnp.float32)
            part = jnp.sum(jnp.where(keep, wide * wide, 0.0), axis=0, keepdims=True)
            at = pl.ds(offs[2 * slot + k], 1)
            sums[at, :] = sums[at, :] + part
        return carry

    lax.fori_loop(0, group, body, 0)


def column_sums(blocks, offs, live, domain):
    slots = blocks.shape[0]
    group = min(16, slots)
    return pl.pallas_call(
        functools.partial(sums_kernel, group),
        out_shape=jax.ShapeDtypeStruct((domain, BLK), jnp.float32),
        grid_spec=pltpu.PrefetchScalarGridSpec(
            num_scalar_prefetch=2,
            grid=(slots // group,),
            in_specs=[
                pl.BlockSpec((group, 1, BLK, BLK), lambda i, *_: (i, 0, 0, 0)),
                pl.BlockSpec((group, 1, BLK, BLK), lambda i, *_: (i, 1, 0, 0)),
            ],
            out_specs=pl.BlockSpec((domain, BLK), lambda i, *_: (0, 0)),
        ),
        compiler_params=pltpu.CompilerParams(vmem_limit_bytes=VMEM_LIMIT),
    )(offs, live, blocks, blocks)


def apply_kernel(first, group, unroll, offs, live, core, blk, scale, own, peer, *rest):
    if first:
        keep, send, scaled, modes, total, sems = rest
    else:
        keep, send, modes, total, sems = rest
    step = pl.program_id(0)
    half = keep.shape[0]
    mine = core[0] * half
    other = (1 - core[0]) * half

    @pl.when(step == 0)
    def _():
        one = pltpu.make_async_copy(own, modes.at[pl.ds(mine, half)], sems.at[0])
        two = pltpu.make_async_copy(peer, modes.at[pl.ds(other, half)], sems.at[1])
        one.start()
        two.start()

        def clear(i, carry):
            total[pl.ds(2 * i, 2)] = jnp.zeros((2,) + total.shape[1:], jnp.float32)
            return carry

        lax.fori_loop(0, half, clear, 0)
        one.wait()
        two.wait()

    rows = lax.broadcasted_iota(jnp.int32, (BLK, BLK), 0)

    def body(g, carry):
        wide, places = [], []
        for u in range(unroll):
            s = g * unroll + u
            slot = step * group + s
            place = [offs[2 * slot], offs[2 * slot + 1]]
            pair = [blk[s, 0], blk[s, 1]]
            if first:
                alive = rows < live[slot]
                for k in range(2):
                    value = pair[k].astype(jnp.float32) * scale[pl.ds(place[k], 1), :]
                    pair[k] = jnp.where(alive, value, 0.0).astype(jnp.bfloat16)
                    scaled[s, k] = pair[k]
            wide.append(jnp.concatenate(pair, axis=1))
            places.append(place)
        picked = [jnp.concatenate([modes[p], modes[q]], axis=1) for p, q in places]
        projected = [nt_dot(v, a).astype(jnp.bfloat16) for v, a in zip(picked, wide)]
        spread = [
            jnp.dot(v, a, preferred_element_type=jnp.float32) for v, a in zip(projected, wide)
        ]
        for (p, q), value in zip(places, spread):
            total[p] += value[:, :BLK]
            total[q] += value[:, BLK:]
        return carry

    lax.fori_loop(0, group // unroll, body, 0)

    @pl.when(step == pl.num_programs(0) - 1)
    def _():
        def write(i, carry):
            keep[pl.ds(2 * i, 2)] = total[pl.ds(mine + 2 * i, 2)].astype(jnp.bfloat16)
            send[pl.ds(2 * i, 2)] = total[pl.ds(other + 2 * i, 2)].astype(jnp.bfloat16)
            return carry

        lax.fori_loop(0, half // 2, write, 0)


def apply_rows(first, blocks, offs, live, core, scale, own, peer):
    slots = blocks.shape[0]
    half, modes, _ = own.shape
    group = min(16, slots)
    unroll = min(8, group)
    block_spec = pl.BlockSpec((group, 2, BLK, BLK), lambda i, *_: (i, 0, 0, 0))
    half_spec = pl.BlockSpec((half, modes, BLK), lambda i, *_: (0, 0, 0))
    half_shape = jax.ShapeDtypeStruct(own.shape, jnp.bfloat16)
    out_shape, out_specs = [half_shape, half_shape], [half_spec, half_spec]
    if first:
        out_shape.append(jax.ShapeDtypeStruct(blocks.shape, jnp.bfloat16))
        out_specs.append(block_spec)
    return pl.pallas_call(
        functools.partial(apply_kernel, first, group, unroll),
        out_shape=out_shape,
        grid_spec=pltpu.PrefetchScalarGridSpec(
            num_scalar_prefetch=3,
            grid=(slots // group,),
            in_specs=[
                block_spec,
                pl.BlockSpec(scale.shape, lambda i, *_: (0, 0)),
                pl.BlockSpec(memory_space=pl.ANY),
                pl.BlockSpec(memory_space=pl.ANY),
            ],
            out_specs=out_specs,
            scratch_shapes=[
                pltpu.VMEM((2 * half, modes, BLK), jnp.bfloat16),
                pltpu.VMEM((2 * half, modes, BLK), jnp.float32),
                pltpu.SemaphoreType.DMA((2,)),
            ],
        ),
        compiler_params=pltpu.CompilerParams(vmem_limit_bytes=VMEM_LIMIT),
        cost_estimate=pl.CostEstimate(
            flops=10**10, bytes_accessed=12 * 10**6, transcendentals=0
        ),
    )(offs, live, core, blocks, scale, own, peer)


def image_kernel(second, with_ritz, *refs):
    one, two, own, damped, *rest = refs
    before = rest.pop(0) if second else None
    own_before = rest.pop(0) if with_ritz else None
    applied, gram = rest[:2]
    ritz = rest[2] if with_ritz else None

    @pl.when(pl.program_id(0) == 0)
    def _():
        gram[...] = jnp.zeros_like(gram)
        if with_ritz:
            ritz[...] = jnp.zeros_like(ritz)

    gram_part = jnp.zeros(gram.shape, jnp.float32)
    ritz_part = jnp.zeros(ritz.shape, jnp.float32) if with_ritz else None
    for i in range(0, one.shape[0], 2):
        values = []
        for l in (i, i + 1):
            total = one[l].astype(jnp.float32) + two[l].astype(jnp.float32)
            old = own[l].astype(jnp.float32)
            value = (total + damped[l] * old).astype(jnp.bfloat16)
            applied[l] = value
            values.append(value)
        value = jnp.concatenate(values, axis=1)
        everything = value
        if second:
            earlier = jnp.concatenate([before[i], before[i + 1]], axis=1)
            everything = jnp.concatenate([earlier, value], axis=0)
        gram_part += nt_dot(value, everything)
        if with_ritz:
            olds = [jnp.concatenate([own_before[l], own[l]], axis=0) for l in (i, i + 1)]
            ritz_part += nt_dot(jnp.concatenate(olds, axis=1), everything)
    gram[...] += gram_part
    if with_ritz:
        ritz[...] += ritz_part


def form_image(one, two, own, damped, before=(), with_ritz=False, steps=3):
    half, modes, _ = own.shape
    part = half // steps
    second = len(before) > 0
    part_spec = pl.BlockSpec((part, modes, BLK), lambda i: (i, 0, 0))
    shapes = [(modes, 2 * modes if second else modes)] + [(2 * modes, 2 * modes)] * with_ritz
    return pl.pallas_call(
        functools.partial(image_kernel, second, with_ritz),
        out_shape=[jax.ShapeDtypeStruct(own.shape, jnp.bfloat16)]
        + [jax.ShapeDtypeStruct(shape, jnp.float32) for shape in shapes],
        grid=(steps,),
        in_specs=[part_spec] * 3
        + [pl.BlockSpec((part, 1, BLK), lambda i: (i, 0, 0))]
        + [part_spec] * len(before),
        out_specs=[part_spec] + [pl.BlockSpec(shape, lambda i: (0, 0)) for shape in shapes],
        compiler_params=pltpu.CompilerParams(vmem_limit_bytes=SMALL_LIMIT),
        cost_estimate=pl.CostEstimate(flops=10**9, bytes_accessed=4 * 10**6, transcendentals=0),
    )(one, two, own, damped, *before)


def exact(left, right, dims):
    return lax.dot_general(
        left, right, (dims, ((), ())), precision=lax.Precision.HIGHEST,
        preferred_element_type=jnp.float32,
    )


def eliminate(work, size, at):
    row_at = lax.broadcasted_iota(jnp.int32, work.shape, 0)
    for j in range(size):
        root = lax.rsqrt(work[j : j + 1, at + j : at + j + 1])
        row = work[j : j + 1, :] * root
        factor = jnp.where(row_at[:, :1] > j, work[:, at + j : at + j + 1] * root, 0.0)
        work = jnp.where(row_at == j, row, work - factor * row)
    return work


def unit(size):
    at = lax.broadcasted_iota(jnp.int32, (size, size), 0)
    return (at == lax.broadcasted_iota(jnp.int32, (size, size), 1)).astype(jnp.float32)


def first_inverse(gram):
    size = gram.shape[0]
    none = jnp.zeros((size, size), jnp.float32)
    work = jnp.concatenate([unit(size), none, gram, none], axis=1)
    return eliminate(work, size, 2 * size)[:, :size]


def second_inverse(gram, first):
    size = first.shape[0]
    cross = exact(gram[:, :size], first, ((1,), (1,)))
    rest = gram[:, size:] - exact(cross, cross, ((1,), (1,)))
    left = -exact(cross, first, ((1,), (0,)))
    none = jnp.zeros((size, size), jnp.float32)
    work = jnp.concatenate([left, unit(size), rest, none], axis=1)
    return eliminate(work, size, 2 * size)[:, : 2 * size]


def first_kernel(gram_one, gram_two, applied, new, first, inverse):
    @pl.when(pl.program_id(0) == 0)
    def _():
        value = first_inverse(gram_one[...] + gram_two[...])
        first[...] = value
        inverse[...] = value.astype(jnp.bfloat16)

    for i in range(0, applied.shape[0], 2):
        pair = jnp.concatenate([applied[i], applied[i + 1]], axis=1)
        value = jnp.dot(inverse[...], pair, preferred_element_type=jnp.float32)
        new[i] = value[:, :BLK].astype(jnp.bfloat16)
        new[i + 1] = value[:, BLK:].astype(jnp.bfloat16)


def second_kernel(upper, gram_one, gram_two, first, before, applied, new, inverse):
    @pl.when(pl.program_id(0) == 0)
    def _():
        value = second_inverse(gram_one[...] + gram_two[...], first[...])
        above = jnp.concatenate([first[...], jnp.zeros_like(first)], axis=1)
        inverse[...] = jnp.where(upper[0] == 1, above, value).astype(jnp.bfloat16)

    for i in range(0, applied.shape[0], 2):
        both = [jnp.concatenate([before[l], applied[l]], axis=0) for l in (i, i + 1)]
        pair = jnp.concatenate(both, axis=1)
        value = jnp.dot(inverse[...], pair, preferred_element_type=jnp.float32)
        new[i] = value[:, :BLK].astype(jnp.bfloat16)
        new[i + 1] = value[:, BLK:].astype(jnp.bfloat16)


def first_modes(gram_one, gram_two, applied, steps=3):
    half, modes, _ = applied.shape
    part_spec = pl.BlockSpec((half // steps, modes, BLK), lambda i: (i, 0, 0))
    square_spec = pl.BlockSpec((modes, modes), lambda i: (0, 0))
    return pl.pallas_call(
        first_kernel,
        out_shape=[
            jax.ShapeDtypeStruct(applied.shape, jnp.bfloat16),
            jax.ShapeDtypeStruct((modes, modes), jnp.float32),
        ],
        grid=(steps,),
        in_specs=[square_spec, square_spec, part_spec],
        out_specs=[part_spec, square_spec],
        scratch_shapes=[pltpu.VMEM((modes, modes), jnp.bfloat16)],
        compiler_params=pltpu.CompilerParams(vmem_limit_bytes=SMALL_LIMIT),
        cost_estimate=pl.CostEstimate(flops=3 * 10**9, bytes_accessed=10**6, transcendentals=0),
    )(gram_one, gram_two, applied)


def second_modes(upper, gram_one, gram_two, first, before, applied, steps=3):
    half, modes, _ = applied.shape
    part_spec = pl.BlockSpec((half // steps, modes, BLK), lambda i, *_: (i, 0, 0))
    rows_spec = pl.BlockSpec((modes, 2 * modes), lambda i, *_: (0, 0))
    square_spec = pl.BlockSpec((modes, modes), lambda i, *_: (0, 0))
    return pl.pallas_call(
        second_kernel,
        out_shape=jax.ShapeDtypeStruct(applied.shape, jnp.bfloat16),
        grid_spec=pltpu.PrefetchScalarGridSpec(
            num_scalar_prefetch=1,
            grid=(steps,),
            in_specs=[rows_spec, rows_spec, square_spec, part_spec, part_spec],
            out_specs=part_spec,
            scratch_shapes=[pltpu.VMEM((modes, 2 * modes), jnp.bfloat16)],
        ),
        compiler_params=pltpu.CompilerParams(vmem_limit_bytes=SMALL_LIMIT),
        cost_estimate=pl.CostEstimate(flops=3 * 10**9, bytes_accessed=10**6, transcendentals=0),
    )(upper, gram_one, gram_two, first, before, applied)


def side(xh, xl):
    return 1 - (xh ^ xl)


def flat(ny, nz, y, z, c, xh, xl):
    return (((y * nz + z) * 2 + c) * 2 + xh) * 2 + xl


def every(ny, nz):
    return [
        (y, z, c, xh, xl)
        for y in range(ny)
        for z in range(nz)
        for c in range(2)
        for xh in range(2)
        for xl in range(2)
    ]


def next_pairs(ny, nz, cross):
    pairs = []
    for y, z, c, xh, xl in every(ny, nz):
        sub = ((y * nz + z) * 2 + side(xh, xl) + 1) % (ny * nz * 2)
        to = xh ^ cross
        there = (sub // (2 * nz), sub // 2 % nz, c, to, to ^ (1 - sub % 2))
        pairs.append((flat(ny, nz, y, z, c, xh, xl), flat(ny, nz, *there)))
    return pairs


def out_pairs(ny, nz, crossed):
    pairs = []
    for y, z, c, xh, xl in every(ny, nz):
        if c != side(xh, xl):
            there = (y, z, 1 - c if crossed else c, xh, 1 - xl)
            pairs.append((flat(ny, nz, *there), flat(ny, nz, y, z, c, xh, xl)))
    return pairs


def spread_pairs():
    return [
        (side(xh, xl) * 4 + xh * 2 + xl, (1 - side(xh, xl)) * 4 + xh * 2 + xl)
        for xh in range(2)
        for xl in range(2)
    ]


def start_pairs(mask):
    return [
        (side(x // 2, x % 2) * 4 + (x ^ mask), side(x // 2, x % 2) * 4 + x) for x in range(4)
    ]


def core_swap(value):
    return lax.ppermute(value, "c", [(0, 1), (1, 0)])


def chip_swap(value):
    return lax.ppermute(value, ("xh", "xl"), [(0, 3), (3, 0), (1, 2), (2, 1)])


def slot_rows(targets, wanted, rows):
    equal = targets[..., None, :] == wanted[:, None]
    at = jnp.arange(rows, dtype=jnp.int32)
    first = jnp.min(jnp.where(equal, at, rows), axis=-1)
    last = jnp.max(jnp.where(equal, at, -1), axis=-1)
    valid = jnp.stack([first < rows, last > first], axis=-1)
    return jnp.where(valid, jnp.stack([first, last], axis=-1), 0), valid


def shards(ny, nz, blocks, routes, offsets, live, start_modes):
    y, z, c, xh, xl = [lax.axis_index(axis) for axis in AXES]
    own_side = 1 - (xh ^ xl)
    subs = ny * nz * 2
    rows = blocks.shape[0]
    domain, share = start_modes.shape[1], start_modes.shape[2]
    half = domain // 2
    group = ("y", "z", "xl")

    targets = routes[:, 0]
    wanted = jnp.arange(subs, dtype=jnp.int32) ^ (1 - xh)
    order, _ = slot_rows(targets, wanted, rows)
    table = jnp.stack([targets, offsets[:, 0], offsets[:, 1], live], axis=0)
    table = jnp.pad(table.astype(jnp.float32), ((0, 4), (0, BLK - rows)))
    packed, table, start_modes = lax.optimization_barrier(
        (pack(blocks, order.reshape(-1)), table, start_modes)
    )
    received = lax.all_to_all(packed, group, split_axis=0, concat_axis=0, tiled=True)

    tables = lax.all_gather(table, AXES, axis=0, tiled=False)[:, :4, :rows]
    tables = tables.astype(jnp.int32).reshape(ny, nz, 2, 2, 2, 4, rows)
    tables = lax.dynamic_index_in_dim(tables, c, 2, keepdims=False)
    tables = lax.dynamic_index_in_dim(tables, xh, 2, keepdims=False).reshape(subs, 4, rows)
    here = ((y * nz + z) * 2 + own_side).astype(jnp.int32)
    index, valid = slot_rows(tables[:, 0, :], here[None], rows)
    index, valid = index[:, 0], valid[:, 0]
    onehot = index[..., None] == jnp.arange(rows, dtype=jnp.int32)
    picked = [
        jnp.sum(jnp.where(onehot & valid[..., None], tables[:, None, k, :], 0), axis=-1)
        for k in (1, 2, 3)
    ]
    offs = jnp.stack(picked[:2], axis=-1).reshape(-1)
    alive = picked[2].reshape(-1)

    by = [start_modes[0]] + [
        lax.ppermute(start_modes[0], ("c", "xh", "xl"), start_pairs(mask)) for mask in (1, 2, 3)
    ]
    quarters = []
    for q in range(4):
        near = [jnp.where(xl == q % 2, by[2 * m], by[2 * m + 1]) for m in range(2)]
        quarters.append(jnp.where(xh == q // 2, near[0], near[1]))
    gathered = jnp.concatenate(quarters, axis=1)
    sibling = lax.ppermute(gathered, ("c", "xh", "xl"), spread_pairs())
    start = jnp.where(c == own_side, gathered, sibling)
    cut = start.shape[1] // 2
    owns, peers = [
        [
            lax.dynamic_slice(start, (at * half, h * cut, 0), (half, cut, BLK))
            for h in range(2)
        ]
        for at in (c, 1 - c)
    ]

    sums = column_sums(received, offs, alive, domain)
    sums = sums + core_swap(sums)
    low, high = [], []
    for cross in range(2):
        forward = next_pairs(ny, nz, cross)
        backward = [(there, here_) for here_, there in forward]
        low.append(lax.ppermute(sums[domain - OV :], AXES, forward))
        high.append(lax.ppermute(sums[:OV], AXES, backward))
    column_sq = (sums + chip_swap(sums)) + jnp.concatenate(
        [low[0] + low[1], jnp.zeros((domain - 2 * OV, BLK), jnp.float32), high[0] + high[1]],
        axis=0,
    )
    scale = lax.rsqrt(column_sq + DAMPING)
    damped = lax.dynamic_slice_in_dim(DAMPING * scale * scale, c * half, half, 0)[:, None, :]

    core = c.astype(jnp.int32)[None]
    def apply_half(h, first=False):
        return apply_rows(first, work, offs, alive, core, scale, owns[h], peers[h])

    def add_cores(keep, send, after=None):
        other = core_swap(send)
        if after is not None:
            keep, _ = lax.optimization_barrier((keep, after))
        return (keep.astype(jnp.float32) + other.astype(jnp.float32)).astype(jnp.bfloat16)

    work = received
    lower = jnp.zeros((1,), jnp.int32)
    keep, send, work = apply_half(0, True)
    one = add_cores(keep, send)
    one, owns[1] = lax.optimization_barrier((one, owns[1]))
    for step in range(ITERS):
        last = step == ITERS - 1
        one_there = chip_swap(one)
        keep, send = apply_half(1)
        one_there, keep = lax.optimization_barrier((one_there, keep))
        before, gram = form_image(one, one_there, owns[0], damped)
        two = add_cores(keep, send, after=gram)
        two_there = chip_swap(two)
        two, gram = lax.optimization_barrier((two, gram))
        new, first = first_modes(gram, core_swap(gram), before)
        if last:
            two_there, first = lax.optimization_barrier((two_there, first))
            applied, gram, ritz = form_image(
                two, two_there, owns[1], damped, (before, owns[0]), True
            )
            upper = (1 - xh).astype(jnp.int32)[None]
            out = second_modes(upper, gram, core_swap(gram), first, before, applied)
        else:
            owns[0], peers[0] = new, core_swap(new)
            keep, send = apply_half(0)
            two_there, keep = lax.optimization_barrier((two_there, keep))
            applied, gram = form_image(two, two_there, owns[1], damped, (before,))
            one = add_cores(keep, send, after=gram)
            one, gram = lax.optimization_barrier((one, gram))
            new = second_modes(lower, gram, core_swap(gram), first, before, applied)
            owns[1], peers[1] = new, core_swap(new)

    at_home = c == own_side
    ritz = ritz + core_swap(ritz)
    ritz = jnp.where(at_home, ritz, lax.ppermute(ritz, AXES, out_pairs(ny, nz, True)))
    mine = lax.dynamic_slice_in_dim(out, xl * share, share, 1)
    beside = lax.dynamic_slice_in_dim(out, (1 - xl) * share, share, 1)
    same = lax.ppermute(beside, AXES, out_pairs(ny, nz, False))
    crossed = lax.ppermute(beside, AXES, out_pairs(ny, nz, True))
    sibling = core_swap(mine)
    this_half = jnp.where(at_home, mine, same)
    other_half = jnp.where(at_home, sibling, crossed)
    low = jnp.where(c == 0, this_half, other_half)
    high = jnp.where(c == 0, other_half, this_half)
    return jnp.concatenate([low, high], axis=0)[None], ritz[None]


def solution(mesh, ny=4):
    nz = mesh.shape["sub"] // (2 * ny)
    grid = Mesh(mesh.devices.reshape(ny, nz, 2, 2, 2), AXES)
    subs, inner = ("y", "z", "c"), ("xh", "xl")
    return jax.shard_map(
        functools.partial(shards, ny, nz),
        mesh=grid,
        in_specs=(
            P(subs + inner, None, None, None),
            P(subs + inner, None),
            P(subs + inner, None),
            P(subs + inner),
            P(subs, None, inner, None),
        ),
        out_specs=(P(subs, None, inner, None), P(subs, None, None)),
        check_vma=False,
    )
```
